32 devices in a mesh: pix: 8 (over z, y), head: 4 (over x, core).
Axes of the slice: x: 2, y: 2, z: 4, core: 2. Of those that a mesh axis runs over, the one named last changes fastest.
Arguments:
- queries: bfloat16 [4096, 1024], P('pix', 'head'), may hold values from -6 to 6
- keys: bfloat16 [4096, 1024], P('pix', 'head'), may hold values from -6 to 6
- values: bfloat16 [4096, 1024], P('pix', 'head'), may hold values from -24 to 24
- coarse_keys: bfloat16 [64, 1024], P('pix', 'head'), may hold values from -6 to 6
- coarse_values: bfloat16 [64, 1024], P('pix', 'head'), may hold values from -24 to 24
- neighbors: int32 [32, 4], P('pix'), may hold values from 0 to 31, as said below
- pool_map: int32 [4096], P('pix'), may hold values from 0 to 63, as said below
- coarse_mask: int32 [32, 8], P('pix'), may hold values 0 or 1
- w_out: bfloat16 [1024, 1024], P('head'), may hold values from -0.1875 to 0.1875
- grad_mixed: bfloat16 [4096, 1024], P('pix', 'head'), may hold values from -48 to 48
Outputs:
- mixed: bfloat16 [4096, 1024], P('pix', 'head')
- grad_queries: bfloat16 [4096, 1024], P('pix', 'head')
- grad_keys: bfloat16 [4096, 1024], P('pix', 'head')
- grad_values: bfloat16 [4096, 1024], P('pix', 'head')
- grad_coarse_keys: float32 [64, 1024], P('pix', 'head')
- grad_coarse_values: float32 [64, 1024], P('pix', 'head')
- grad_w_out: float32 [1024, 1024], P('head')
The draws below stay inside these ranges and needn't reach their ends.
Inputs may be any that keep to these rules, and one draw needn't show every extreme that they name: `neighbors`: row b starts with b itself, followed by 4 - 1 different blocks b + o with 1 <= |o| <= 2; where b + o falls outside 0 to 31, b - o stands in its place, so that entries may repeat near the two ends. `pool_map`: the fine pixels of slab s (rows s * 512 to (s + 1) * 512 - 1) map into coarse rows s * 8 to (s + 1) * 8 - 1, and the first 8 pixels of each slab name each of those rows once.
All inputs are finite; a program needn't handle non-finite values. No bound on the sum of `coarse_mask` on one device may be relied on, other than what follows from the above.
Results may differ from the reference program's by a relative error of at most 0.018.
Values may be sent and summed in bfloat16 or wider, within the bound.
No kernel may reach another device: no remote copies, remote signals or barrier semaphores. Data moves between devices by JAX's collectives and lax.ppermute only.
A program may use at most 64 MiB of HBM per device.

```python
import jax
import jax.numpy as jnp
from jax import lax

HEADS = 16
HDIM = 64
D = 1024
BLK = 128
NBR = 4
HB = 2
CBLK = 8
TOK_DEV = 512
CR_DEV = 8
TOKENS = 4096
COARSE = 64
NBLK = 32
CBT = 8


def attention_pair(key):
    base = jax.random.fold_in(key, 7)
    shape = (TOKENS, D)
    query = jax.random.truncated_normal(jax.random.fold_in(base, 1), -6.0, 6.0, shape, jnp.float32)
    keyed = jax.random.truncated_normal(jax.random.fold_in(base, 2), -6.0, 6.0, shape, jnp.float32)
    return (query, keyed)


def draw_queries(key, part):
    return attention_pair(key)[0].astype(jnp.bfloat16)


def draw_keys(key, part):
    return attention_pair(key)[1].astype(jnp.bfloat16)


def draw_neighbors(key, part):
    count = TOKENS // BLK
    offsets = jnp.concatenate([jnp.arange(-HB, 0), jnp.arange(1, HB + 1)]).astype(jnp.int32)
    row_keys = jax.random.split(jax.random.fold_in(key, 21), count)

    def one_order(row_key):
        return jax.random.permutation(row_key, 2 * HB)
    orders = jax.vmap(one_order)(row_keys)
    picked = offsets[orders[:, :NBR - 1]]
    block = jnp.arange(count, dtype=jnp.int32)[:, None]
    target = block + picked
    target = jnp.where((target < 0) | (target >= count), block - picked, target)
    return jnp.concatenate([block, target], axis=1).astype(jnp.int32)


def draw_pool_map(key, part):
    slabs = TOKENS // TOK_DEV
    slab_keys = jax.random.split(jax.random.fold_in(key, 31), slabs)

    def one_order(slab_key):
        return jax.random.permutation(slab_key, CR_DEV)
    orders = jax.vmap(one_order)(slab_keys)
    rows = jnp.arange(TOKENS, dtype=jnp.int32)
    slab_index = rows // TOK_DEV
    position = rows % TOK_DEV
    spread = jax.random.randint(jax.random.fold_in(key, 32), (TOKENS,), 0, CR_DEV)
    first = orders[slab_index, jnp.minimum(position, CR_DEV - 1)]
    chosen = jnp.where(position < CR_DEV, first, spread)
    return (slab_index * CR_DEV + chosen).astype(jnp.int32)


def touch_ends(values, key, smallest, largest):
    longest = values.shape.index(max(values.shape))
    spots = []
    for shift in (0, 1):
        where = [jax.random.randint(jax.random.fold_in(key, axis), (), 0, length) for axis, length in enumerate(values.shape)]
        where[longest] = (where[longest] + shift) % values.shape[longest]
        spots.append(tuple(where))
    return values.at[spots[0]].set(smallest).at[spots[1]].set(largest)


def levels(own_key, dims, cuts, smallest, top_value):
    loudness = 1.0
    for dim, parts in cuts:
        heights = jax.random.uniform(jax.random.fold_in(jax.random.fold_in(own_key, 6), dim), (parts,), jnp.float32, smallest / len(cuts), top_value / len(cuts))
        loudness = loudness * jnp.repeat(jnp.exp(heights), dims[dim] // parts).reshape((-1,) + (1,) * (len(dims) - 1 - dim))
    return loudness


def scatter_about(key, shape, width, bound, pieces=(), kind=jnp.bfloat16):
    result = jax.random.normal(key, shape, jnp.float32) * width
    if len(pieces) > 0:
        result = levels(key, shape, pieces, -0.22, 0.18) * result
    return jnp.clip(result, min=-bound, max=bound).astype(kind)


def setup_inputs(seed: int = 0) -> dict:
    key_list = jax.random.split(jax.random.key(seed), 11)
    queries = draw_queries(jax.random.fold_in(key_list[10], 71), 0)
    keys = draw_keys(jax.random.fold_in(key_list[10], 71), 0)
    values = scatter_about(key_list[2], (TOKENS, D), 4.0, 24.0, ((0, 8), (1, 4)))
    coarse_keys = scatter_about(key_list[3], (COARSE, D), 1.0, 6.0, ((0, 8), (1, 4)))
    coarse_values = scatter_about(key_list[4], (COARSE, D), 4.0, 24.0, ((0, 8), (1, 4)))
    neighbors = draw_neighbors(jax.random.fold_in(key_list[10], 71), 0)
    pool_map = draw_pool_map(jax.random.fold_in(key_list[10], 71), 0)
    coarse_mask = touch_ends((jax.random.randint(key_list[7], (NBLK, CBT), 0, 2) < 1).astype(jnp.int32), jax.random.fold_in(key_list[7], 1), 0, 1)
    w_out = scatter_about(key_list[8], (D, D), D ** -0.5, 0.1875, ((0, 4),))
    grad_mixed = scatter_about(key_list[9], (TOKENS, D), 8.0, 48.0, ((0, 8), (1, 4)))
    return dict(queries=queries, keys=keys, values=values, coarse_keys=coarse_keys, coarse_values=coarse_values, neighbors=neighbors, pool_map=pool_map, coarse_mask=coarse_mask, w_out=w_out, grad_mixed=grad_mixed)


def rounded(array):
    return lax.optimization_barrier(array.astype(jnp.bfloat16)).astype(jnp.float32)


def reference(queries, keys, values, coarse_keys, coarse_values, neighbors, pool_map, coarse_mask, w_out, grad_mixed):
    score_scale = HDIM ** -0.5
    heads = HEADS
    slabs = TOKENS // TOK_DEV
    per_slab = TOK_DEV // BLK
    counts = jax.ops.segment_sum(jnp.ones((TOKENS,), jnp.float32), pool_map, num_segments=COARSE)
    sums = jax.ops.segment_sum(jnp.concatenate([keys, values], 1).astype(jnp.float32), pool_map, num_segments=COARSE)
    means = sums / counts[:, None]
    panel_k = (means[:, :D] + coarse_keys.astype(jnp.float32)).astype(jnp.bfloat16)
    panel_v = (means[:, D:] + coarse_values.astype(jnp.float32)).astype(jnp.bfloat16)
    panel_keys = panel_k.astype(jnp.float32).reshape(COARSE, heads, HDIM)
    panel_values = panel_v.astype(jnp.float32).reshape(COARSE, heads, HDIM)
    padding = HB * BLK
    key_blocks = jnp.pad(keys, ((padding, padding), (0, 0))).reshape(NBLK + 2 * HB, BLK, heads, HDIM)
    value_blocks = jnp.pad(values, ((padding, padding), (0, 0))).reshape(NBLK + 2 * HB, BLK, heads, HDIM)
    grad_attn = jnp.dot(grad_mixed, w_out.T, preferred_element_type=jnp.float32).astype(jnp.bfloat16)
    allowed = jnp.repeat(coarse_mask > 0, CBLK, axis=1).reshape(slabs, per_slab, COARSE)
    query_slabs = queries.reshape(slabs, per_slab, BLK, heads, HDIM)
    grad_slabs = grad_attn.reshape(slabs, per_slab, BLK, heads, HDIM)
    listed = (neighbors + HB).astype(jnp.int32).reshape(slabs, per_slab, NBR)

    def slab_step(carry, inputs):
        fine_k_grad, fine_v_grad, coarse_grad = carry
        query, grad_out, picks, allowed_rows = inputs
        query = query.astype(jnp.float32)
        grad_out = grad_out.astype(jnp.float32)
        fine_keys = key_blocks[picks].reshape(per_slab, NBR * BLK, heads, HDIM).astype(jnp.float32)
        fine_values = value_blocks[picks].reshape(per_slab, NBR * BLK, heads, HDIM).astype(jnp.float32)
        fine_scores = score_scale * jnp.einsum("nbhd,nmhd->nhbm", query, fine_keys)
        coarse_scores = score_scale * jnp.einsum("nbhd,rhd->nhbr", query, panel_keys)
        coarse_scores = jnp.where(allowed_rows[:, None, None, :], coarse_scores, -jnp.inf)
        maxima = jnp.maximum(jnp.max(fine_scores, -1), jnp.max(coarse_scores, -1))
        fine_exp = jnp.exp(fine_scores - maxima[..., None])
        coarse_exp = jnp.exp(coarse_scores - maxima[..., None])
        totals = jnp.sum(fine_exp, -1) + jnp.sum(coarse_exp, -1)
        fine_w = fine_exp / totals[..., None]
        coarse_w = coarse_exp / totals[..., None]
        fine_wb = rounded(fine_w)
        coarse_wb = rounded(coarse_w)
        attn_sum = jnp.einsum("nhbm,nmhd->nbhd", fine_wb, fine_values) + jnp.einsum("nhbr,rhd->nbhd", coarse_wb, panel_values)
        attn_b = lax.optimization_barrier(attn_sum.astype(jnp.bfloat16))
        attn_f = attn_b.astype(jnp.float32)
        dterm = jnp.einsum("nbhd,nbhd->nhb", grad_out, attn_f)
        fine_ds = rounded(fine_w * (jnp.einsum("nbhd,nmhd->nhbm", grad_out, fine_values) - dterm[..., None]))
        coarse_ds = rounded(coarse_w * (jnp.einsum("nbhd,rhd->nhbr", grad_out, panel_values) - dterm[..., None]))
        grad_query = score_scale * (jnp.einsum("nhbm,nmhd->nbhd", fine_ds, fine_keys) + jnp.einsum("nhbr,rhd->nbhd", coarse_ds, panel_keys))
        flat = picks.reshape(-1)
        fine_k_grad = fine_k_grad.at[flat].add((score_scale * jnp.einsum("nhbm,nbhd->nmhd", fine_ds, query)).reshape(per_slab * NBR, BLK, heads, HDIM))
        fine_v_grad = fine_v_grad.at[flat].add(jnp.einsum("nhbm,nbhd->nmhd", fine_wb, grad_out).reshape(per_slab * NBR, BLK, heads, HDIM))
        coarse_terms = jnp.stack([score_scale * jnp.einsum("nhbr,nbhd->rhd", coarse_ds, query), jnp.einsum("nhbr,nbhd->rhd", coarse_wb, grad_out)])
        coarse_grad = coarse_grad + coarse_terms
        return (fine_k_grad, fine_v_grad, coarse_grad), (attn_b, grad_query.astype(jnp.bfloat16))

    start = (jnp.zeros((NBLK + 2 * HB, BLK, heads, HDIM), jnp.float32), jnp.zeros((NBLK + 2 * HB, BLK, heads, HDIM), jnp.float32), jnp.zeros((2, COARSE, heads, HDIM), jnp.float32))
    finals, outputs = lax.scan(slab_step, start, (query_slabs, grad_slabs, listed, allowed))
    fine_k_grad, fine_v_grad, coarse_grad = finals
    attn = outputs[0].reshape(TOKENS, D)
    grad_queries = outputs[1].reshape(TOKENS, D)
    mixed = jnp.dot(attn, w_out, preferred_element_type=jnp.float32).astype(jnp.bfloat16)
    grad_w_out = jnp.dot(attn.T, grad_mixed, preferred_element_type=jnp.float32) * (TOKENS ** -0.5)
    grad_coarse = coarse_grad.reshape(2, COARSE, D)
    per_row = grad_coarse / counts[None, :, None]
    grad_keys = (fine_k_grad[HB:HB + NBLK].reshape(TOKENS, D) + per_row[0][pool_map]).astype(jnp.bfloat16)
    grad_values = (fine_v_grad[HB:HB + NBLK].reshape(TOKENS, D) + per_row[1][pool_map]).astype(jnp.bfloat16)
    return (mixed, grad_queries, grad_keys, grad_values, grad_coarse[0], grad_coarse[1], grad_w_out)
```

```python
import functools
import math

import jax
import jax.numpy as jnp
from jax import lax
from jax.experimental import pallas as pl
from jax.experimental.pallas import tpu as pltpu
from jax.sharding import PartitionSpec as P

HDIM = 64
BLK = 128
NBR = 4
HB = 2
CBLK = 8
RIM = HB * BLK
SCALE = HDIM ** (-0.5)
LOG2E = math.log2(math.e)
BF = jnp.bfloat16
F32 = jnp.float32
VMEM = pl.BlockSpec(memory_space=pltpu.VMEM)
SMEM = pl.BlockSpec(memory_space=pltpu.SMEM)


def mm(a, b):
    return jnp.dot(a, b, preferred_element_type=F32)


def mm_t(a, b):
    return lax.dot_general(a, b, (((1,), (1,)), ((), ())), preferred_element_type=F32)


def t_mm(a, b):
    return lax.dot_general(a, b, (((0,), (0,)), ((), ())), preferred_element_type=F32)


def bit_list(count):
    return [1 << i for i in range(count.bit_length() - 1)]


def swap(value, axis, bit):
    return lax.ppermute(value, axis, [(i, i ^ bit) for i in range(lax.axis_size(axis))])


def reversed_bits(index, levels):
    out = 0
    for level in range(levels):
        out = out * 2 + ((index >> level) & 1)
    return out


def call(body, outs, scratch=(), smem=(), count=0, flops=0, bytes_accessed=0):
    return pl.pallas_call(
        body,
        out_shape=[jax.ShapeDtypeStruct(s, t) for s, t in outs],
        in_specs=[SMEM if i in smem else VMEM for i in range(count)],
        out_specs=[VMEM] * len(outs),
        scratch_shapes=list(scratch),
        compiler_params=pltpu.CompilerParams(vmem_limit_bytes=48 * 1024 * 1024),
        cost_estimate=pl.CostEstimate(
            flops=flops, bytes_accessed=bytes_accessed, transcendentals=0
        ),
    )


def membership(pool_ref, rows):
    me = lax.axis_index("pix")
    local = pool_ref[...] - me * rows
    count = pool_ref.shape[1]
    return local == lax.broadcasted_iota(jnp.int32, (rows, count), 0)


def prep_kernel(k_ref, v_ref, ck_ref, cv_ref, pool_ref, lo_ref, hi_ref, panel_ref):
    tok = k_ref.shape[0]
    lo_ref[0:RIM] = k_ref[0:RIM]
    lo_ref[RIM:] = v_ref[0:RIM]
    hi_ref[0:RIM] = k_ref[tok - RIM :]
    hi_ref[RIM:] = v_ref[tok - RIM :]
    member = membership(pool_ref, ck_ref.shape[0]).astype(F32)
    counts = jnp.sum(member, axis=1, keepdims=True)
    member = member.astype(BF)
    panel_k = mm(member, k_ref[...]) / counts + ck_ref[...].astype(F32)
    panel_v = mm(member, v_ref[...]) / counts + cv_ref[...].astype(F32)
    panel_ref[...] = jnp.concatenate([panel_k, panel_v], 0).astype(BF)


def grad_kernel(*refs):
    pieces, w_ref, go_ref = refs[:-2], refs[-2], refs[-1]
    me = lax.axis_index("head")
    width = w_ref.shape[0]
    total = None
    for j, ref in enumerate(pieces):
        w = w_ref[:, pl.ds(pl.multiple_of((me ^ j) * width, width), width)]
        part = mm_t(ref[...], w)
        total = part if total is None else total + part
    go_ref[...] = total.astype(BF)


def head_masks(width, rows):
    lane = lax.broadcasted_iota(jnp.int32, (rows, width), 1)
    return [(lane >= h * HDIM) & (lane < (h + 1) * HDIM) for h in range(width // HDIM)]


def stacked(block, masks):
    zero = jnp.zeros_like(block)
    return jnp.concatenate([jnp.where(m, block, zero) for m in masks], 0)


def unstacked(tall, masks):
    rows = tall.shape[0] // len(masks)
    out = tall[0:rows]
    for h in range(1, len(masks)):
        out = jnp.where(masks[h], tall[h * rows : (h + 1) * rows], out)
    return out


def extend(ext_k, ext_v, k_ref, v_ref, prev_ref, next_ref):
    tok = k_ref.shape[0]
    ext_k[0:RIM] = prev_ref[0:RIM]
    ext_v[0:RIM] = prev_ref[RIM:]
    ext_k[RIM : RIM + tok] = k_ref[...]
    ext_v[RIM : RIM + tok] = v_ref[...]
    ext_k[RIM + tok :] = next_ref[0:RIM]
    ext_v[RIM + tok :] = next_ref[RIM:]


def panel_parts(panel_ref, rows):
    width = panel_ref.shape[1]
    slots = panel_ref.shape[0] // (2 * rows)
    both = panel_ref[...].astype(F32).reshape(slots, 2 * rows, width)
    keys = both[:, :rows].reshape(slots * rows, width).astype(BF)
    values = both[:, rows:].reshape(slots * rows, width).astype(BF)
    return keys, values


def picks(nbr_ref, block, blocks):
    me = lax.axis_index("pix")
    starts = []
    for n in range(NBR):
        index = nbr_ref[block, n] - me * blocks + HB
        starts.append(pl.multiple_of(index * BLK, BLK))
    return starts


def gathered(ext, starts, panel):
    return jnp.concatenate([ext[pl.ds(s, BLK), :] for s in starts] + [panel], 0)


def forward_kernel(rows, levels, pieces_count, *refs):
    (nbr_ref, mask_ref, q_ref, k_ref, v_ref, prev_ref, next_ref, panel_ref, w_ref) = refs[:9]
    pieces = refs[9 : 9 + pieces_count]
    (attn_ref, p_ref, mix_keep, mix_send, gw_keep, gw_send, ext_k, ext_v, gw_all) = refs[
        9 + pieces_count :
    ]
    tok, width = q_ref.shape
    blocks = tok // BLK
    me = lax.axis_index("pix")
    me_head = lax.axis_index("head")
    extend(ext_k, ext_v, k_ref, v_ref, prev_ref, next_ref)
    panel_k, panel_v = panel_parts(panel_ref, rows)
    coarse = panel_k.shape[0]
    cols = mask_ref.shape[1]
    row = lax.broadcasted_iota(jnp.int32, (cols, coarse), 1)
    owner_row = ((row // rows) ^ me) * rows + row % rows
    pick = (owner_row // CBLK) == lax.broadcasted_iota(jnp.int32, (cols, coarse), 0)
    allowed = mm((mask_ref[...] > 0).astype(BF), pick.astype(BF))
    masks = head_masks(width, BLK)
    for b in range(blocks):
        starts = picks(nbr_ref, b, blocks)
        q_tall = stacked(q_ref[b * BLK : (b + 1) * BLK], masks)
        scores = mm_t(q_tall, gathered(ext_k, starts, panel_k)) * (SCALE * LOG2E)
        fine = scores[:, : NBR * BLK]
        lo = jnp.where(allowed[b : b + 1] > 0.5, scores[:, NBR * BLK :], -jnp.inf)
        top = jnp.maximum(
            jnp.max(fine, axis=1, keepdims=True), jnp.max(lo, axis=1, keepdims=True)
        )
        fine = jnp.exp2(fine - top)
        lo = jnp.exp2(lo - top)
        total = jnp.sum(fine, axis=1, keepdims=True) + jnp.sum(lo, axis=1, keepdims=True)
        scale = 1.0 / total
        weights = jnp.concatenate([fine * scale, lo * scale], 1).astype(BF)
        p_ref[b] = weights
        out = mm(weights, gathered(ext_v, starts, panel_v))
        attn_ref[b * BLK : (b + 1) * BLK] = unstacked(out, masks).astype(BF)
    attn = attn_ref[...]
    for j in range(pieces_count):
        w = w_ref[:, pl.ds(pl.multiple_of((me_head ^ j) * width, width), width)]
        part = mm(attn, w).astype(BF)
        target = mix_send if j & 1 else mix_keep
        target[(j >> 1) * tok : ((j >> 1) + 1) * tok] = part
    chunk = width >> levels
    mine = reversed_bits(me, levels)
    for j in range(pieces_count):
        part = t_mm(attn, pieces[j][...]).astype(BF)
        lanes = pl.ds(pl.multiple_of((me_head ^ j) * width, width), width)
        for c in range(1 << levels):
            place = pl.ds(pl.multiple_of((c ^ mine) * chunk, chunk), chunk)
            gw_all[place, lanes] = part[c * chunk : (c + 1) * chunk]
    gw_keep[...] = gw_all[: width // 2]
    gw_send[...] = gw_all[width // 2 :]


def backward_kernel(rows, *refs):
    (nbr_ref, q_ref, k_ref, v_ref, prev_ref, next_ref, panel_ref, go_ref, attn_ref, p_ref) = refs[
        :10
    ]
    (dq_ref, own_ref, to_prev, to_next, coarse_ref, ext_k, ext_v, sum_k, sum_v) = refs[10:]
    tok, width = q_ref.shape
    blocks = tok // BLK
    extend(ext_k, ext_v, k_ref, v_ref, prev_ref, next_ref)
    panel_k, panel_v = panel_parts(panel_ref, rows)
    coarse = panel_k.shape[0]
    masks = head_masks(width, BLK)
    sum_k[...] = jnp.zeros_like(sum_k)
    sum_v[...] = jnp.zeros_like(sum_v)
    coarse_k = jnp.zeros((coarse, width), F32)
    coarse_v = jnp.zeros((coarse, width), F32)
    heads = len(masks)
    for b in range(blocks):
        span = slice(b * BLK, (b + 1) * BLK)
        starts = picks(nbr_ref, b, blocks)
        q_tall = stacked(q_ref[span], masks)
        g_tall = stacked(go_ref[span], masks)
        attn = attn_ref[span].astype(F32)
        dterm = jnp.sum(
            g_tall.astype(F32) * jnp.concatenate([attn] * heads, 0), axis=1, keepdims=True
        )
        weights = p_ref[b]
        slope = mm_t(g_tall, gathered(ext_v, starts, panel_v))
        ds = (weights.astype(F32) * (slope - dterm)).astype(BF)
        dq = unstacked(mm(ds, gathered(ext_k, starts, panel_k)), masks)
        dq_ref[span] = (SCALE * dq).astype(BF)
        dk = SCALE * t_mm(ds, q_tall)
        dv = t_mm(weights, g_tall)
        for n in range(NBR):
            place = pl.ds(starts[n], BLK)
            sum_k[place, :] += dk[n * BLK : (n + 1) * BLK]
            sum_v[place, :] += dv[n * BLK : (n + 1) * BLK]
        coarse_k = coarse_k + dk[NBR * BLK :]
        coarse_v = coarse_v + dv[NBR * BLK :]
    own_ref[0:tok] = sum_k[RIM : RIM + tok]
    own_ref[tok:] = sum_v[RIM : RIM + tok]
    to_prev[0:RIM] = sum_k[0:RIM].astype(BF)
    to_prev[RIM:] = sum_v[0:RIM].astype(BF)
    to_next[0:RIM] = sum_k[RIM + tok :].astype(BF)
    to_next[RIM:] = sum_v[RIM + tok :].astype(BF)
    for j in range(coarse // rows):
        coarse_ref[2 * j * rows : (2 * j + 1) * rows] = coarse_k[j * rows : (j + 1) * rows]
        coarse_ref[(2 * j + 1) * rows : (2 * j + 2) * rows] = coarse_v[j * rows : (j + 1) * rows]


def finish_kernel(own_ref, below_ref, above_ref, coarse_ref, pool_ref, gk_ref, gv_ref, ck_ref, cv_ref):
    tok, width = gk_ref.shape
    rows = ck_ref.shape[0]
    member = membership(pool_ref, rows).astype(F32)
    counts = jnp.sum(member, axis=1, keepdims=True)
    member = member.astype(BF)
    ck_ref[...] = coarse_ref[0:rows]
    cv_ref[...] = coarse_ref[rows:]
    member = jnp.concatenate([member, member], 0)
    for which, out in ((0, gk_ref), (1, gv_ref)):
        per_row = coarse_ref[which * rows : (which + 1) * rows] / counts
        high = per_row.astype(BF)
        low = (per_row - high.astype(F32)).astype(BF)
        pooled = t_mm(member, jnp.concatenate([high, low], 0))
        grads = own_ref[which * tok : (which + 1) * tok] + pooled
        half = slice(which * RIM, (which + 1) * RIM)
        head = grads[0:RIM] + below_ref[half].astype(F32)
        tail = grads[tok - RIM :] + above_ref[half].astype(F32)
        if tok >= 2 * RIM:
            out[0:RIM] = head.astype(BF)
            if tok > 2 * RIM:
                out[RIM : tok - RIM] = grads[RIM : tok - RIM].astype(BF)
            out[tok - RIM :] = tail.astype(BF)


def gw_kernel(levels, factor, in_ref, out_ref):
    me = lax.axis_index("pix")
    width = out_ref.shape[0]
    chunk = width >> levels
    mine = reversed_bits(me, levels)
    for c in range(1 << levels):
        place = pl.ds(pl.multiple_of((c ^ mine) * chunk, chunk), chunk)
        out_ref[c * chunk : (c + 1) * chunk] = in_ref[place, :].astype(F32) * factor


def on_device(
    queries,
    keys,
    values,
    coarse_keys,
    coarse_values,
    neighbors,
    pool_map,
    coarse_mask,
    w_out,
    grad_mixed,
):
    tok, width = queries.shape
    rows = coarse_keys.shape[0]
    pix = lax.axis_size("pix")
    head = lax.axis_size("head")
    blocks = tok // BLK
    coarse = pix * rows
    d_model = head * width
    bits = bit_list(pix)
    head_bits = bit_list(head)
    levels = min(2, len(bits))
    heads = width // HDIM
    forward_pairs = [(i, i + 1) for i in range(pix - 1)]
    backward_pairs = [(i + 1, i) for i in range(pix - 1)]
    pool_row = pool_map.reshape(1, tok)

    order = [grad_mixed]
    index = [0]
    for bit in reversed(head_bits):
        order = order + [swap(piece, "head", bit) for piece in order]
        index = index + [i ^ bit for i in index]
    grads = [order[index.index(j)] for j in range(head)]

    lo, hi, panel = call(
        prep_kernel,
        [((2 * RIM, width), BF), ((2 * RIM, width), BF), ((2 * rows, width), BF)],
        count=5,
        flops=4 * rows * tok * width,
        bytes_accessed=4 * tok * width * 2,
    )(keys, values, coarse_keys, coarse_values, pool_row)
    prev = lax.ppermute(hi, "pix", forward_pairs)
    nxt = lax.ppermute(lo, "pix", backward_pairs)
    for bit in bits:
        panel = jnp.concatenate([panel, swap(panel, "pix", bit)], 0)

    (grad_attn,) = call(
        grad_kernel,
        [((tok, width), BF)],
        count=head + 1,
        flops=2 * tok * width * d_model,
        bytes_accessed=(2 * tok * d_model + width * d_model) * 2,
    )(*grads, w_out)

    keys_each = NBR * BLK + coarse
    tall = heads * BLK
    product = 2 * tall * keys_each * width
    attn, weights, mix_keep, mix_send, gw_keep, gw_send = call(
        functools.partial(forward_kernel, rows, levels, head),
        [
            ((tok, width), BF),
            ((blocks, tall, keys_each), BF),
            ((head // 2 * tok, width), BF),
            ((head // 2 * tok, width), BF),
            ((width // 2, d_model), BF),
            ((width // 2, d_model), BF),
        ],
        scratch=[
            pltpu.VMEM((tok + 2 * RIM, width), BF),
            pltpu.VMEM((tok + 2 * RIM, width), BF),
            pltpu.VMEM((width, d_model), BF),
        ],
        smem=(0,),
        count=9 + head,
        flops=2 * blocks * product + 4 * tok * width * d_model,
        bytes_accessed=10_000_000,
    )(neighbors, coarse_mask, queries, keys, values, prev, nxt, panel, w_out, *grads)

    kept, sent = mix_keep, mix_send
    for bit in head_bits:
        total = kept.astype(F32) + swap(sent, "head", bit).astype(F32)
        if kept.shape[0] > tok:
            half = kept.shape[0] // 2
            kept, sent = total[:half], total[half:].astype(BF)
    mixed = total.astype(BF)

    kept, sent = gw_keep, gw_send
    for level, bit in enumerate(bits):
        if level >= levels:
            sent = kept.astype(BF)
        total = kept.astype(F32) + swap(sent, "pix", bit).astype(F32)
        if level + 1 < levels:
            half = total.shape[0] // 2
            kept, sent = total[:half], total[half:].astype(BF)
        else:
            kept = total
    part = kept.astype(BF)
    for bit in reversed(bits[:levels]):
        part = jnp.concatenate([part, swap(part, "pix", bit)], 0)
    (grad_w_out,) = call(
        functools.partial(gw_kernel, levels, (tok * pix) ** (-0.5)),
        [((width, d_model), F32)],
        count=1,
        flops=0,
        bytes_accessed=6 * width * d_model,
    )(part)

    grad_queries, own, to_prev, to_next, coarse_grads = call(
        functools.partial(backward_kernel, rows),
        [
            ((tok, width), BF),
            ((2 * tok, width), F32),
            ((2 * RIM, width), BF),
            ((2 * RIM, width), BF),
            ((2 * coarse, width), F32),
        ],
        scratch=[
            pltpu.VMEM((tok + 2 * RIM, width), BF),
            pltpu.VMEM((tok + 2 * RIM, width), BF),
            pltpu.VMEM((tok + 2 * RIM, width), F32),
            pltpu.VMEM((tok + 2 * RIM, width), F32),
        ],
        smem=(0,),
        count=10,
        flops=4 * blocks * product,
        bytes_accessed=10_000_000,
    )(neighbors, queries, keys, values, prev, nxt, panel, grad_attn, attn, weights)

    above = lax.ppermute(to_prev, "pix", backward_pairs)
    below = lax.ppermute(to_next, "pix", forward_pairs)
    for bit in reversed(bits):
        half = coarse_grads.shape[0] // 2
        coarse_grads = coarse_grads[:half] + swap(coarse_grads[half:], "pix", bit)

    grad_keys, grad_values, grad_ck, grad_cv = call(
        finish_kernel,
        [((tok, width), BF), ((tok, width), BF), ((rows, width), F32), ((rows, width), F32)],
        count=5,
        flops=8 * rows * tok * width,
        bytes_accessed=16 * tok * width,
    )(own, below, above, coarse_grads, pool_row)
    return (mixed, grad_queries, grad_keys, grad_values, grad_ck, grad_cv, grad_w_out)


def solution(mesh):
    in_specs = (
        P("pix", "head"),
        P("pix", "head"),
        P("pix", "head"),
        P("pix", "head"),
        P("pix", "head"),
        P("pix", None),
        P("pix"),
        P("pix", None),
        P("head", None),
        P("pix", "head"),
    )
    out_specs = (
        P("pix", "head"),
        P("pix", "head"),
        P("pix", "head"),
        P("pix", "head"),
        P("pix", "head"),
        P("pix", "head"),
        P("head", None),
    )
    return jax.shard_map(
        on_device, mesh=mesh, in_specs=in_specs, out_specs=out_specs, check_vma=False
    )
```

```python
import functools
import math

import jax
import jax.numpy as jnp
from jax import lax
from jax.experimental import pallas as pl
from jax.experimental.pallas import tpu as pltpu
from jax.sharding import PartitionSpec as P

HDIM = 64
BLK = 128
NBR = 4
HB = 2
CBLK = 8
RIM = HB * BLK
SCALE = HDIM ** (-0.5)
LOG2E = math.log2(math.e)
BF = jnp.bfloat16
F32 = jnp.float32
VMEM = pl.BlockSpec(memory_space=pltpu.VMEM)
HBM = pl.BlockSpec(memory_space=pltpu.HBM)


def mm(a, b):
    return jnp.dot(a, b, preferred_element_type=F32)


def mm_t(a, b):
    return lax.dot_general(a, b, (((1,), (1,)), ((), ())), preferred_element_type=F32)


def t_mm(a, b):
    return lax.dot_general(a, b, (((0,), (0,)), ((), ())), preferred_element_type=F32)


def bit_list(count):
    return [1 << i for i in range(count.bit_length() - 1)]


def swap(value, axis, bit):
    return lax.ppermute(value, axis, [(i, i ^ bit) for i in range(lax.axis_size(axis))])


def exchange(value, pairs):
    return lax.ppermute(value, "pix", pairs + [(b, a) for a, b in pairs])


def near_pairs(count):
    return [(i, i + 1) for i in range(0, count, 2)]


def far_pairs(count):
    return [(i, i + 1) for i in range(1, count - 1, 2)]


def gather_parts(value, bits):
    offsets = [0]
    for bit in bits:
        offsets = offsets + [o + bit for o in offsets]
    return [value if o == 0 else swap(value, "pix", o) for o in offsets]


def gather_bits(value, bits):
    return jnp.concatenate(gather_parts(value, bits), 0)


def cut(lines, height, width, count):
    across = lines.shape[1] // width
    cells = []
    for t in range(count):
        top, left = t // across * height, t % across * width
        cells.append(lines[top : top + height, left : left + width])
    return cells


def reversed_bits(index, levels):
    out = 0
    for level in range(levels):
        out = out * 2 + ((index >> level) & 1)
    return out


def call(body, outs, specs, out_specs=None, scratch=(), flops=0, bytes_accessed=0):
    return pl.pallas_call(
        body,
        out_shape=[jax.ShapeDtypeStruct(s, t) for s, t in outs],
        in_specs=list(specs),
        out_specs=[VMEM] * len(outs) if out_specs is None else list(out_specs),
        scratch_shapes=list(scratch),
        compiler_params=pltpu.CompilerParams(vmem_limit_bytes=48 * 1024 * 1024),
        cost_estimate=pl.CostEstimate(
            flops=flops, bytes_accessed=bytes_accessed, transcendentals=0
        ),
    )


def membership(pool_ref, rows):
    me = lax.axis_index("pix")
    local = pool_ref[...] - me * rows
    count = pool_ref.shape[1]
    return local == lax.broadcasted_iota(jnp.int32, (rows, count), 0)


def prep_kernel(
    k_hbm, v_hbm, ck_hbm, cv_hbm, pool_hbm, mask_hbm,
    k_ref, v_ref, near_ref, far_ref, panel_ref, pool_ref, mask_ref,
    ck_ref, cv_ref, sems,
):
    tok = k_ref.shape[0]
    odd = lax.axis_index("pix") & 1
    near = pl.ds(pl.multiple_of((1 - odd) * (tok - RIM), RIM), RIM)
    far = pl.ds(pl.multiple_of(odd * (tok - RIM), RIM), RIM)
    pairs = [
        (pool_hbm, pool_ref),
        (k_hbm, k_ref),
        (v_hbm, v_ref),
        (ck_hbm, ck_ref),
        (cv_hbm, cv_ref),
        (k_hbm.at[near], near_ref.at[pl.ds(0, RIM)]),
        (v_hbm.at[near], near_ref.at[pl.ds(RIM, RIM)]),
        (k_hbm.at[far], far_ref.at[pl.ds(0, RIM)]),
        (v_hbm.at[far], far_ref.at[pl.ds(RIM, RIM)]),
        (mask_hbm, mask_ref),
    ]
    copies = [pltpu.make_async_copy(x, y, sems.at[i]) for i, (x, y) in enumerate(pairs)]
    for copy in copies:
        copy.start()
    for copy in copies[:5]:
        copy.wait()
    member = membership(pool_ref, ck_ref.shape[0]).astype(F32)
    counts = jnp.sum(member, axis=1, keepdims=True)
    member = member.astype(BF)
    panel_k = mm(member, k_ref[...]) / counts + ck_ref[...].astype(F32)
    panel_v = mm(member, v_ref[...]) / counts + cv_ref[...].astype(F32)
    panel_ref[...] = jnp.concatenate([panel_k, panel_v], 0).astype(BF)
    for copy in copies[5:]:
        copy.wait()


def grad_kernel(gm_hbm, q_hbm, w_hbm, *refs):
    pieces = refs[:-5]
    go_ref, gm_ref, q_ref, w_ref, sems = refs[-5:]
    copies = [
        pltpu.make_async_copy(x, y, sems.at[i])
        for i, (x, y) in enumerate([(w_hbm, w_ref), (gm_hbm, gm_ref), (q_hbm, q_ref)])
    ]
    for copy in copies:
        copy.start()
    me = lax.axis_index("head")
    width = w_ref.shape[0]
    copies[0].wait()
    copies[1].wait()
    total = None
    for j, ref in enumerate((gm_ref,) + pieces):
        w = w_ref[:, pl.ds(pl.multiple_of((me ^ j) * width, width), width)]
        part = mm_t(ref[...], w)
        total = part if total is None else total + part
    go_ref[...] = total.astype(BF)
    copies[2].wait()


def head_masks(width, rows):
    lane = lax.broadcasted_iota(jnp.int32, (rows, width), 1)
    return [(lane >= h * HDIM) & (lane < (h + 1) * HDIM) for h in range(width // HDIM)]


def stacked(block, masks):
    zero = jnp.zeros_like(block)
    return jnp.concatenate([jnp.where(m, block, zero) for m in masks], 0)


def unstacked(tall, masks):
    rows = tall.shape[0] // len(masks)
    out = tall[0:rows]
    for h in range(1, len(masks)):
        out = jnp.where(masks[h], tall[h * rows : (h + 1) * rows], out)
    return out


def extend(ext_k, ext_v, k_ref, v_ref, near_ref, far_ref):
    tok = k_ref.shape[0]
    odd = lax.axis_index("pix") & 1
    ext_k[RIM : RIM + tok] = k_ref[...]
    ext_v[RIM : RIM + tok] = v_ref[...]
    near = pl.ds(pl.multiple_of((1 - odd) * (tok + RIM), RIM), RIM)
    far = pl.ds(pl.multiple_of(odd * (tok + RIM), RIM), RIM)
    ext_k[near, :] = near_ref[0:RIM]
    ext_v[near, :] = near_ref[RIM:]
    ext_k[far, :] = far_ref[0:RIM]
    ext_v[far, :] = far_ref[RIM:]


def panel_parts(panel_ref, rows):
    width = panel_ref.shape[1]
    slots = panel_ref.shape[0] // (2 * rows)
    both = panel_ref[...].astype(F32).reshape(slots, 2 * rows, width)
    keys = both[:, :rows].reshape(slots * rows, width).astype(BF)
    values = both[:, rows:].reshape(slots * rows, width).astype(BF)
    return keys, values


def picks(nbr_ref, block, blocks):
    me = lax.axis_index("pix")
    starts = []
    for n in range(NBR):
        index = nbr_ref[block, n] - me * blocks + HB
        starts.append(pl.multiple_of(index * BLK, BLK))
    return starts


def gathered(ext, starts, panel):
    return jnp.concatenate([ext[pl.ds(s, BLK), :] for s in starts] + [panel], 0)


def forward_kernel(rows, levels, *refs):
    (nbr_hbm, mask_ref, q_ref, k_ref, v_ref, near_ref, far_ref, panel_ref, w_ref, go_ref) = refs[
        :10
    ]
    outs = len(refs) - 13
    pieces = refs[10:outs]
    (attn_ref, p_hbm, mix_keep, mix_send, gw_keep, gw_send) = refs[outs : outs + 6]
    (nbr_ref, ext_k, ext_v, gw_all, p_ref, nbr_sem, p_sems) = refs[outs + 6 :]
    tok, width = q_ref.shape
    blocks = tok // BLK
    fetch = pltpu.make_async_copy(nbr_hbm, nbr_ref, nbr_sem)
    fetch.start()
    me = lax.axis_index("pix")
    me_head = lax.axis_index("head")
    extend(ext_k, ext_v, k_ref, v_ref, near_ref, far_ref)
    panel_k, panel_v = panel_parts(panel_ref, rows)
    coarse = panel_k.shape[0]
    cols = mask_ref.shape[1]
    row = lax.broadcasted_iota(jnp.int32, (cols, coarse), 1)
    owner_row = ((row // rows) ^ me) * rows + row % rows
    pick = (owner_row // CBLK) == lax.broadcasted_iota(jnp.int32, (cols, coarse), 0)
    allowed = mm((mask_ref[...] > 0).astype(BF), pick.astype(BF))
    masks = head_masks(width, BLK)
    heads = len(masks)
    coarse_k = jnp.zeros((coarse, width), F32)
    coarse_v = jnp.zeros((coarse, width), F32)
    fetch.wait()
    stores = []
    for b in range(blocks):
        span = slice(b * BLK, (b + 1) * BLK)
        starts = picks(nbr_ref, b, blocks)
        q_tall = stacked(q_ref[span], masks)
        scores = mm_t(q_tall, gathered(ext_k, starts, panel_k)) * (SCALE * LOG2E)
        fine = scores[:, : NBR * BLK]
        lo = jnp.where(allowed[b : b + 1] > 0.5, scores[:, NBR * BLK :], -jnp.inf)
        top = jnp.maximum(
            jnp.max(fine, axis=1, keepdims=True), jnp.max(lo, axis=1, keepdims=True)
        )
        fine = jnp.exp2(fine - top)
        lo = jnp.exp2(lo - top)
        total = jnp.sum(fine, axis=1, keepdims=True) + jnp.sum(lo, axis=1, keepdims=True)
        scale = 1.0 / total
        coarse_w = (lo * scale).astype(BF)
        weights = jnp.concatenate([(fine * scale).astype(BF), coarse_w], 1)
        p_ref[b] = weights
        store = pltpu.make_async_copy(p_ref.at[b], p_hbm.at[b], p_sems.at[b])
        store.start()
        stores.append(store)
        attn = unstacked(mm(weights, gathered(ext_v, starts, panel_v)), masks).astype(BF)
        attn_ref[span] = attn
        g_tall = stacked(go_ref[span], masks)
        dterm = row_terms(g_tall, attn, heads)
        coarse_ds = coarse_w.astype(F32) * (mm_t(g_tall, panel_v) - dterm)
        coarse_k = coarse_k + t_mm(coarse_ds.astype(BF), q_tall)
        coarse_v = coarse_v + t_mm(coarse_w, g_tall)
    coarse_k = coarse_k * SCALE
    attn = attn_ref[...]
    for j, piece in enumerate(pieces):
        lanes = pl.ds(pl.multiple_of((me_head ^ j) * width, width), width)
        part = mm(attn, w_ref[:, lanes]).astype(BF)
        target = mix_send if j & 1 else mix_keep
        target[(j >> 1) * tok : ((j >> 1) + 1) * tok] = part
    chunk = width >> levels
    mine = reversed_bits(me, levels)
    for j, piece in enumerate(pieces):
        part = t_mm(attn, piece[...]).astype(BF)
        lanes = pl.ds(pl.multiple_of((me_head ^ j) * width, width), width)
        for c in range(1 << levels):
            place = pl.ds(pl.multiple_of((c ^ mine) * chunk, chunk), chunk)
            gw_all[place, lanes] = part[c * chunk : (c + 1) * chunk]
    segment = gw_keep.shape[0] * 2 >> levels
    across = gw_all.shape[1] // width
    if (coarse // rows) >> levels < across:
        for target in (gw_keep, gw_send):
            target[...] = jnp.zeros_like(target)
    for s in range(1 << levels):
        target = gw_keep if s < (1 << levels) // 2 else gw_send
        base = (s % ((1 << levels) // 2)) * segment
        target[base : base + chunk] = gw_all[s * chunk : (s + 1) * chunk]
    for j in range(coarse // rows):
        s = reversed_bits(j, levels)
        t = j >> levels
        target = gw_keep if s < (1 << levels) // 2 else gw_send
        base = (s % ((1 << levels) // 2)) * segment + chunk + (t // across) * 2 * rows
        lanes = slice((t % across) * width, (t % across + 1) * width)
        both = [coarse_k[j * rows : (j + 1) * rows], coarse_v[j * rows : (j + 1) * rows]]
        target[base : base + 2 * rows, lanes] = jnp.concatenate(both, 0).astype(BF)
    for store in stores:
        store.wait()


def row_terms(g_tall, attn, heads):
    tall = jnp.concatenate([attn.astype(F32)] * heads, 0)
    return jnp.sum(g_tall.astype(F32) * tall, axis=1, keepdims=True)


def backward_kernel(rows, *refs):
    (nbr_hbm, q_ref, k_ref, v_ref, near_ref, far_ref, panel_ref, go_ref, attn_ref, p_hbm) = refs[
        :10
    ]
    (dq_ref, own_ref, to_near, to_far) = refs[10:14]
    (nbr_ref, ext_k, ext_v, sum_k, sum_v, p_ref, nbr_sem, p_sems) = refs[14:]
    tok, width = q_ref.shape
    blocks = tok // BLK
    fetch = pltpu.make_async_copy(nbr_hbm, nbr_ref, nbr_sem)
    fetch.start()
    loads = [
        pltpu.make_async_copy(p_hbm.at[b], p_ref.at[b], p_sems.at[b]) for b in range(blocks)
    ]
    for load in loads:
        load.start()
    odd = lax.axis_index("pix") & 1
    extend(ext_k, ext_v, k_ref, v_ref, near_ref, far_ref)
    panel_k, panel_v = panel_parts(panel_ref, rows)
    masks = head_masks(width, BLK)
    sum_k[...] = jnp.zeros_like(sum_k)
    sum_v[...] = jnp.zeros_like(sum_v)
    heads = len(masks)
    fetch.wait()
    for b in range(blocks):
        span = slice(b * BLK, (b + 1) * BLK)
        starts = picks(nbr_ref, b, blocks)
        q_tall = stacked(q_ref[span], masks)
        g_tall = stacked(go_ref[span], masks)
        dterm = row_terms(g_tall, attn_ref[span], heads)
        slope = mm_t(g_tall, gathered(ext_v, starts, panel_v))
        loads[b].wait()
        weights = p_ref[b]
        ds = (weights.astype(F32) * (slope - dterm)).astype(BF)
        dq = unstacked(mm(ds, gathered(ext_k, starts, panel_k)), masks)
        dq_ref[span] = (SCALE * dq).astype(BF)
        dk = SCALE * t_mm(ds[:, : NBR * BLK], q_tall)
        dv = t_mm(weights[:, : NBR * BLK], g_tall)
        for n in range(NBR):
            place = pl.ds(starts[n], BLK)
            sum_k[place, :] += dk[n * BLK : (n + 1) * BLK]
            sum_v[place, :] += dv[n * BLK : (n + 1) * BLK]
    own_ref[0:tok] = sum_k[RIM : RIM + tok]
    own_ref[tok:] = sum_v[RIM : RIM + tok]
    near = pl.ds(pl.multiple_of((1 - odd) * (tok + RIM), RIM), RIM)
    far = pl.ds(pl.multiple_of(odd * (tok + RIM), RIM), RIM)
    to_near[0:RIM] = sum_k[near, :].astype(BF)
    to_near[RIM:] = sum_v[near, :].astype(BF)
    to_far[0:RIM] = sum_k[far, :].astype(BF)
    to_far[RIM:] = sum_v[far, :].astype(BF)


def finish_kernel(
    own_ref, near_ref, far_ref, coarse_ref, pool_ref, gk_ref, gv_ref, ck_ref, cv_ref, acc_ref
):
    tok, width = gk_ref.shape
    rows = ck_ref.shape[0]
    odd = lax.axis_index("pix") & 1
    member = membership(pool_ref, rows).astype(F32)
    counts = jnp.sum(member, axis=1, keepdims=True)
    member = member.astype(BF)
    ck_ref[...] = coarse_ref[0:rows]
    cv_ref[...] = coarse_ref[rows:]
    member = jnp.concatenate([member, member], 0)
    near = pl.ds(pl.multiple_of((1 - odd) * (tok - RIM), RIM), RIM)
    far = pl.ds(pl.multiple_of(odd * (tok - RIM), RIM), RIM)
    for which, out in ((0, gk_ref), (1, gv_ref)):
        per_row = coarse_ref[which * rows : (which + 1) * rows] / counts
        high = per_row.astype(BF)
        low = (per_row - high.astype(F32)).astype(BF)
        pooled = t_mm(member, jnp.concatenate([high, low], 0))
        acc_ref[...] = own_ref[which * tok : (which + 1) * tok] + pooled
        half = slice(which * RIM, (which + 1) * RIM)
        acc_ref[near, :] += near_ref[half].astype(F32)
        acc_ref[far, :] += far_ref[half].astype(F32)
        out[...] = acc_ref[...].astype(BF)


def gw_kernel(levels, factor, *refs):
    out_ref = refs[-1]
    me = lax.axis_index("pix")
    chunk = out_ref.shape[0] >> levels
    mine = reversed_bits(me, levels)
    for slot, ref in enumerate(refs[:-1]):
        place = pl.ds(pl.multiple_of((slot ^ mine) * chunk, chunk), chunk)
        out_ref[place, :] = ref[...].astype(F32) * factor


def on_device(
    queries,
    keys,
    values,
    coarse_keys,
    coarse_values,
    neighbors,
    pool_map,
    coarse_mask,
    w_out,
    grad_mixed,
):
    tok, width = queries.shape
    rows = coarse_keys.shape[0]
    pix = lax.axis_size("pix")
    head = lax.axis_size("head")
    blocks = tok // BLK
    coarse = pix * rows
    d_model = head * width
    bits = bit_list(pix)
    head_bits = bit_list(head)
    levels = min(2, len(bits))
    heads = width // HDIM
    pool_row = pool_map.reshape(1, tok)
    keys_hbm, values_hbm, ck_hbm, cv_hbm, pool_hbm, mask_hbm, nbr_hbm, gm_hbm, q_hbm, w_hbm = [
        pltpu.with_memory_space_constraint(x, pltpu.HBM)
        for x in (
            keys,
            values,
            coarse_keys,
            coarse_values,
            pool_row,
            coarse_mask,
            neighbors,
            grad_mixed,
            queries,
            w_out,
        )
    ]
    across = head
    slots = 1 << levels
    held = (pix // slots + across - 1) // across * 2 * rows
    chunk = width // slots
    segment = chunk + held

    k_own, v_own, send_near, send_far, panel, pool_own, mask_own = call(
        prep_kernel,
        [
            ((tok, width), BF),
            ((tok, width), BF),
            ((2 * RIM, width), BF),
            ((2 * RIM, width), BF),
            ((2 * rows, width), BF),
            ((1, tok), jnp.int32),
            (coarse_mask.shape, jnp.int32),
        ],
        [HBM] * 6,
        scratch=[
            pltpu.VMEM((rows, width), BF),
            pltpu.VMEM((rows, width), BF),
            pltpu.SemaphoreType.DMA((10,)),
        ],
        flops=4 * rows * tok * width,
        bytes_accessed=4 * tok * width * 2,
    )(keys_hbm, values_hbm, ck_hbm, cv_hbm, pool_hbm, mask_hbm)

    grad_early, panel = lax.optimization_barrier((grad_mixed, panel))
    near = exchange(send_near, near_pairs(pix))
    panel = gather_bits(panel, bits[:1])
    first = None
    for at in range(1, len(bits), 2):
        parts = gather_parts(panel, bits[at : at + 2])
        if first is None and len(parts) > 1:
            parts[1], send_far = lax.optimization_barrier((parts[1], send_far))
            first = parts[1]
        panel = jnp.concatenate(parts, 0)
    far = exchange(send_far, far_pairs(pix))

    order = [grad_early]
    index = [0]
    for bit in reversed(head_bits):
        if len(order) > 1:
            order = list(lax.optimization_barrier(tuple(order)))
        order = order + [swap(piece, "head", bit) for piece in order]
        index = index + [i ^ bit for i in index]
    grads = [order[index.index(j)] for j in range(1, head)]
    grad_attn, gm_own, q_own, w_own = call(
        grad_kernel,
        [((tok, width), BF), ((tok, width), BF), ((tok, width), BF), ((width, d_model), BF)],
        [HBM] * 3 + [VMEM] * (head - 1),
        scratch=[pltpu.SemaphoreType.DMA((3,))],
        flops=2 * tok * width * d_model,
        bytes_accessed=(2 * tok * d_model + width * d_model) * 2,
    )(gm_hbm, q_hbm, w_hbm, *grads)

    keys_each = NBR * BLK + coarse
    tall = heads * BLK
    product = 2 * tall * keys_each * width
    attn, weights, mix_keep, mix_send, gw_keep, gw_send = call(
        functools.partial(forward_kernel, rows, levels),
        [
            ((tok, width), BF),
            ((blocks, tall, keys_each), BF),
            ((head // 2 * tok, width), BF),
            ((head // 2 * tok, width), BF),
            ((slots // 2 * segment, d_model), BF),
            ((slots // 2 * segment, d_model), BF),
        ],
        [HBM] + [VMEM] * (9 + head),
        out_specs=[VMEM, HBM] + [VMEM] * 4,
        scratch=[
            pltpu.SMEM(neighbors.shape, jnp.int32),
            pltpu.VMEM((tok + 2 * RIM, width), BF),
            pltpu.VMEM((tok + 2 * RIM, width), BF),
            pltpu.VMEM((width, d_model), BF),
            pltpu.VMEM((blocks, tall, keys_each), BF),
            pltpu.SemaphoreType.DMA,
            pltpu.SemaphoreType.DMA((blocks,)),
        ],
        flops=2 * blocks * product + 4 * tok * width * d_model,
        bytes_accessed=10_000_000,
    )(
        nbr_hbm, mask_own, q_own, k_own, v_own, near, far, panel, w_own, grad_attn, gm_own, *grads
    )

    grad_queries, own, to_near, to_far = call(
        functools.partial(backward_kernel, rows),
        [
            ((tok, width), BF),
            ((2 * tok, width), F32),
            ((2 * RIM, width), BF),
            ((2 * RIM, width), BF),
        ],
        [HBM] + [VMEM] * 8 + [HBM],
        scratch=[
            pltpu.SMEM(neighbors.shape, jnp.int32),
            pltpu.VMEM((tok + 2 * RIM, width), BF),
            pltpu.VMEM((tok + 2 * RIM, width), BF),
            pltpu.VMEM((tok + 2 * RIM, width), F32),
            pltpu.VMEM((tok + 2 * RIM, width), F32),
            pltpu.VMEM((blocks, tall, keys_each), BF),
            pltpu.SemaphoreType.DMA,
            pltpu.SemaphoreType.DMA((blocks,)),
        ],
        flops=4 * blocks * product,
        bytes_accessed=10_000_000,
    )(nbr_hbm, q_own, k_own, v_own, near, far, panel, grad_attn, attn, pltpu.with_memory_space_constraint(weights, pltpu.HBM))

    kept, sent = gw_keep, gw_send
    for level in range(levels):
        got = swap(sent, "pix", bits[level])
        if level == 0:
            got, to_near, to_far = lax.optimization_barrier((got, to_near, to_far))
        total = kept.astype(F32) + got.astype(F32)
        half = total.shape[0] // 2
        if level + 1 < levels:
            kept, sent = total[:half], total[half:].astype(BF)
            sent, to_near, to_far = lax.optimization_barrier((sent, to_near, to_far))
    whole = total
    cells = cut(whole[chunk:], 2 * rows, width, pix // slots)
    part = whole[:chunk]
    for bit in bits[levels:]:
        got = swap(whole.astype(BF), "pix", bit).astype(F32)
        part = part + got[:chunk]
        other = cut(got[chunk:], 2 * rows, width, len(cells))
        cells = [cells[t] + other[t ^ 1] for t in range(0, len(cells), 2)]
        if len(cells) > 1:
            empty = [jnp.zeros_like(cells[0])] * (-len(cells) % across)
            full = cells + empty
            lines = [
                jnp.concatenate(full[t : t + across], 1) for t in range(0, len(full), across)
            ]
            whole = jnp.concatenate([part] + lines, 0)
    coarse_grads = cells[0]
    part = part.astype(BF)
    gathered_parts = [part]
    for bit in reversed(bits[:levels]):
        gathered_parts = gathered_parts + [swap(p, "pix", bit) for p in gathered_parts]
    (grad_w_out,) = call(
        functools.partial(gw_kernel, levels, (tok * pix) ** (-0.5)),
        [((width, d_model), F32)],
        [VMEM] * slots,
        flops=0,
        bytes_accessed=6 * width * d_model,
    )(*gathered_parts)

    kept, sent = mix_keep, mix_send
    for bit in head_bits:
        total = kept.astype(F32) + swap(sent, "head", bit).astype(F32)
        if kept.shape[0] > tok:
            half = kept.shape[0] // 2
            kept, sent = total[:half], total[half:].astype(BF)
    mixed = total.astype(BF)

    got_near = exchange(to_near, near_pairs(pix))
    got_far = exchange(to_far, far_pairs(pix))
    grad_keys, grad_values, grad_ck, grad_cv = call(
        finish_kernel,
        [((tok, width), BF), ((tok, width), BF), ((rows, width), F32), ((rows, width), F32)],
        [VMEM] * 5,
        scratch=[pltpu.VMEM((tok, width), F32)],
        flops=8 * rows * tok * width,
        bytes_accessed=16 * tok * width,
    )(own, got_near, got_far, coarse_grads, pool_own)
    return (mixed, grad_queries, grad_keys, grad_values, grad_ck, grad_cv, grad_w_out)


def solution(mesh):
    in_specs = (
        P("pix", "head"),
        P("pix", "head"),
        P("pix", "head"),
        P("pix", "head"),
        P("pix", "head"),
        P("pix", None),
        P("pix"),
        P("pix", None),
        P("head", None),
        P("pix", "head"),
    )
    out_specs = (
        P("pix", "head"),
        P("pix", "head"),
        P("pix", "head"),
        P("pix", "head"),
        P("pix", "head"),
        P("pix", "head"),
        P("head", None),
    )
    return jax.shard_map(
        on_device, mesh=mesh, in_specs=in_specs, out_specs=out_specs, check_vma=False
    )
```

```python
import functools
import math

import jax
import jax.numpy as jnp
from jax import lax
from jax.experimental import pallas as pl
from jax.experimental.pallas import tpu as pltpu
from jax.sharding import PartitionSpec as P

HDIM = 64
BLK = 128
NBR = 4
HB = 2
CBLK = 8
RIM = HB * BLK
SCALE = HDIM ** (-0.5)
LOG2E = math.log2(math.e)
BF = jnp.bfloat16
F32 = jnp.float32
VMEM = pl.BlockSpec(memory_space=pltpu.VMEM)
HBM = pl.BlockSpec(memory_space=pltpu.HBM)


def mm(a, b):
    return jnp.dot(a, b, preferred_element_type=F32)


def mm_t(a, b):
    return lax.dot_general(a, b, (((1,), (1,)), ((), ())), preferred_element_type=F32)


def t_mm(a, b):
    return lax.dot_general(a, b, (((0,), (0,)), ((), ())), preferred_element_type=F32)


def bit_list(count):
    return [1 << i for i in range(count.bit_length() - 1)]


def swap(value, axis, bit):
    return lax.ppermute(value, axis, [(i, i ^ bit) for i in range(lax.axis_size(axis))])


def exchange(value, pairs):
    return lax.ppermute(value, "pix", pairs + [(b, a) for a, b in pairs])


def near_pairs(count):
    return [(i, i + 1) for i in range(0, count, 2)]


def far_pairs(count):
    return [(i, i + 1) for i in range(1, count - 1, 2)]


def gather_parts(value, bits):
    offsets = [0]
    for bit in bits:
        offsets = offsets + [o + bit for o in offsets]
    return [value if o == 0 else swap(value, "pix", o) for o in offsets]


def gather_bits(value, bits):
    return jnp.concatenate(gather_parts(value, bits), 0)


def cut(lines, height, width, count):
    across = lines.shape[1] // width
    cells = []
    for t in range(count):
        top, left = t // across * height, t % across * width
        cells.append(lines[top : top + height, left : left + width])
    return cells


def reversed_bits(index, levels):
    out = 0
    for level in range(levels):
        out = out * 2 + ((index >> level) & 1)
    return out


def call(body, outs, specs, out_specs=None, scratch=(), flops=0, bytes_accessed=0):
    return pl.pallas_call(
        body,
        out_shape=[jax.ShapeDtypeStruct(s, t) for s, t in outs],
        in_specs=list(specs),
        out_specs=[VMEM] * len(outs) if out_specs is None else list(out_specs),
        scratch_shapes=list(scratch),
        compiler_params=pltpu.CompilerParams(vmem_limit_bytes=48 * 1024 * 1024),
        cost_estimate=pl.CostEstimate(
            flops=flops, bytes_accessed=bytes_accessed, transcendentals=0
        ),
    )


def membership(pool_ref, rows):
    me = lax.axis_index("pix")
    local = pool_ref[...] - me * rows
    count = pool_ref.shape[1]
    return local == lax.broadcasted_iota(jnp.int32, (rows, count), 0)


def prep_kernel(
    k_hbm, v_hbm, ck_hbm, cv_hbm, pool_hbm,
    k_ref, v_ref, panel_ref, pool_ref,
    ck_ref, cv_ref, sems,
):
    pairs = [
        (pool_hbm, pool_ref),
        (k_hbm, k_ref),
        (v_hbm, v_ref),
        (ck_hbm, ck_ref),
        (cv_hbm, cv_ref),
    ]
    copies = [pltpu.make_async_copy(x, y, sems.at[i]) for i, (x, y) in enumerate(pairs)]
    for copy in copies:
        copy.start()
    for copy in copies:
        copy.wait()
    member = membership(pool_ref, ck_ref.shape[0]).astype(F32)
    counts = jnp.sum(member, axis=1, keepdims=True)
    member = member.astype(BF)
    panel_k = mm(member, k_ref[...]) / counts + ck_ref[...].astype(F32)
    panel_v = mm(member, v_ref[...]) / counts + cv_ref[...].astype(F32)
    panel_ref[...] = jnp.concatenate([panel_k, panel_v], 0).astype(BF)


def rim_kernel(k_ref, v_ref, panel_ref, near_ref, far_ref):
    tok = k_ref.shape[0]
    odd = lax.axis_index("pix") & 1
    near = pl.ds(pl.multiple_of((1 - odd) * (tok - RIM), RIM), RIM)
    far = pl.ds(pl.multiple_of(odd * (tok - RIM), RIM), RIM)
    near_ref[0:RIM] = k_ref[near, :]
    near_ref[RIM:] = v_ref[near, :]
    far_ref[0:RIM] = k_ref[far, :]
    far_ref[RIM:] = v_ref[far, :]


def load_kernel(*refs):
    count = len(refs) // 2
    sems = refs[-1]
    copies = [
        pltpu.make_async_copy(refs[i], refs[count + i], sems.at[i]) for i in range(count)
    ]
    for copy in copies:
        copy.start()
    for copy in copies:
        copy.wait()


def grad_kernel(w_ref, *refs):
    pieces, go_ref = refs[:-1], refs[-1]
    me = lax.axis_index("head")
    width = w_ref.shape[0]
    total = None
    for j, ref in enumerate(pieces):
        w = w_ref[:, pl.ds(pl.multiple_of((me ^ j) * width, width), width)]
        part = mm_t(ref[...], w)
        total = part if total is None else total + part
    go_ref[...] = total.astype(BF)


def head_masks(width, rows):
    lane = lax.broadcasted_iota(jnp.int32, (rows, width), 1)
    return [(lane >= h * HDIM) & (lane < (h + 1) * HDIM) for h in range(width // HDIM)]


def stacked(block, masks):
    zero = jnp.zeros_like(block)
    return jnp.concatenate([jnp.where(m, block, zero) for m in masks], 0)


def unstacked(tall, masks):
    rows = tall.shape[0] // len(masks)
    out = tall[0:rows]
    for h in range(1, len(masks)):
        out = jnp.where(masks[h], tall[h * rows : (h + 1) * rows], out)
    return out


def extend(ext_k, ext_v, k_ref, v_ref, near_ref, far_ref):
    tok = k_ref.shape[0]
    odd = lax.axis_index("pix") & 1
    ext_k[RIM : RIM + tok] = k_ref[...]
    ext_v[RIM : RIM + tok] = v_ref[...]
    near = pl.ds(pl.multiple_of((1 - odd) * (tok + RIM), RIM), RIM)
    far = pl.ds(pl.multiple_of(odd * (tok + RIM), RIM), RIM)
    ext_k[near, :] = near_ref[0:RIM]
    ext_v[near, :] = near_ref[RIM:]
    ext_k[far, :] = far_ref[0:RIM]
    ext_v[far, :] = far_ref[RIM:]


def panel_parts(panel_ref, rows):
    width = panel_ref.shape[1]
    slots = panel_ref.shape[0] // (2 * rows)
    both = panel_ref[...].astype(F32).reshape(slots, 2 * rows, width)
    keys = both[:, :rows].reshape(slots * rows, width).astype(BF)
    values = both[:, rows:].reshape(slots * rows, width).astype(BF)
    return keys, values


def picks(nbr_ref, block, blocks):
    me = lax.axis_index("pix")
    starts = []
    for n in range(NBR):
        index = nbr_ref[block, n] - me * blocks + HB
        starts.append(pl.multiple_of(index * BLK, BLK))
    return starts


def gathered(ext, starts, panel):
    return jnp.concatenate([ext[pl.ds(s, BLK), :] for s in starts] + [panel], 0)


def forward_kernel(rows, levels, *refs):
    (nbr_hbm, mask_ref, q_ref, k_ref, v_ref, near_ref, far_ref, panel_ref, w_ref, go_ref) = refs[
        :10
    ]
    outs = len(refs) - 13
    pieces = refs[10:outs]
    (attn_ref, p_hbm, mix_keep, mix_send, gw_keep, gw_send) = refs[outs : outs + 6]
    (nbr_ref, ext_k, ext_v, gw_all, p_ref, nbr_sem, p_sems) = refs[outs + 6 :]
    tok, width = q_ref.shape
    blocks = tok // BLK
    fetch = pltpu.make_async_copy(nbr_hbm, nbr_ref, nbr_sem)
    fetch.start()
    me = lax.axis_index("pix")
    me_head = lax.axis_index("head")
    extend(ext_k, ext_v, k_ref, v_ref, near_ref, far_ref)
    panel_k, panel_v = panel_parts(panel_ref, rows)
    coarse = panel_k.shape[0]
    cols = mask_ref.shape[1]
    row = lax.broadcasted_iota(jnp.int32, (cols, coarse), 1)
    owner_row = ((row // rows) ^ me) * rows + row % rows
    pick = (owner_row // CBLK) == lax.broadcasted_iota(jnp.int32, (cols, coarse), 0)
    allowed = mm((mask_ref[...] > 0).astype(BF), pick.astype(BF))
    masks = head_masks(width, BLK)
    heads = len(masks)
    coarse_k = jnp.zeros((coarse, width), F32)
    coarse_v = jnp.zeros((coarse, width), F32)
    fetch.wait()
    stores = []
    for b in range(blocks):
        span = slice(b * BLK, (b + 1) * BLK)
        starts = picks(nbr_ref, b, blocks)
        q_tall = stacked(q_ref[span], masks)
        scores = mm_t(q_tall, gathered(ext_k, starts, panel_k)) * (SCALE * LOG2E)
        fine = scores[:, : NBR * BLK]
        lo = jnp.where(allowed[b : b + 1] > 0.5, scores[:, NBR * BLK :], -jnp.inf)
        top = jnp.maximum(
            jnp.max(fine, axis=1, keepdims=True), jnp.max(lo, axis=1, keepdims=True)
        )
        fine = jnp.exp2(fine - top)
        lo = jnp.exp2(lo - top)
        total = jnp.sum(fine, axis=1, keepdims=True) + jnp.sum(lo, axis=1, keepdims=True)
        scale = 1.0 / total
        coarse_w = (lo * scale).astype(BF)
        weights = jnp.concatenate([(fine * scale).astype(BF), coarse_w], 1)
        p_ref[b] = weights
        store = pltpu.make_async_copy(p_ref.at[b], p_hbm.at[b], p_sems.at[b])
        store.start()
        stores.append(store)
        attn = unstacked(mm(weights, gathered(ext_v, starts, panel_v)), masks).astype(BF)
        attn_ref[span] = attn
        g_tall = stacked(go_ref[span], masks)
        dterm = row_terms(g_tall, attn, heads)
        coarse_ds = coarse_w.astype(F32) * (mm_t(g_tall, panel_v) - dterm)
        coarse_k = coarse_k + t_mm(coarse_ds.astype(BF), q_tall)
        coarse_v = coarse_v + t_mm(coarse_w, g_tall)
    coarse_k = coarse_k * SCALE
    attn = attn_ref[...]
    for j, piece in enumerate(pieces):
        lanes = pl.ds(pl.multiple_of((me_head ^ j) * width, width), width)
        part = mm(attn, w_ref[:, lanes]).astype(BF)
        target = mix_send if j & 1 else mix_keep
        target[(j >> 1) * tok : ((j >> 1) + 1) * tok] = part
    chunk = width >> levels
    mine = reversed_bits(me, levels)
    for j, piece in enumerate(pieces):
        part = t_mm(attn, piece[...]).astype(BF)
        lanes = pl.ds(pl.multiple_of((me_head ^ j) * width, width), width)
        for c in range(1 << levels):
            place = pl.ds(pl.multiple_of((c ^ mine) * chunk, chunk), chunk)
            gw_all[place, lanes] = part[c * chunk : (c + 1) * chunk]
    segment = gw_keep.shape[0] * 2 >> levels
    across = gw_all.shape[1] // width
    if (coarse // rows) >> levels < across:
        for target in (gw_keep, gw_send):
            target[...] = jnp.zeros_like(target)
    for s in range(1 << levels):
        target = gw_keep if s < (1 << levels) // 2 else gw_send
        base = (s % ((1 << levels) // 2)) * segment
        target[base : base + chunk] = gw_all[s * chunk : (s + 1) * chunk]
    for j in range(coarse // rows):
        s = reversed_bits(j, levels)
        t = j >> levels
        target = gw_keep if s < (1 << levels) // 2 else gw_send
        base = (s % ((1 << levels) // 2)) * segment + chunk + (t // across) * 2 * rows
        lanes = slice((t % across) * width, (t % across + 1) * width)
        both = [coarse_k[j * rows : (j + 1) * rows], coarse_v[j * rows : (j + 1) * rows]]
        target[base : base + 2 * rows, lanes] = jnp.concatenate(both, 0).astype(BF)
    for store in stores:
        store.wait()


def row_terms(g_tall, attn, heads):
    tall = jnp.concatenate([attn.astype(F32)] * heads, 0)
    return jnp.sum(g_tall.astype(F32) * tall, axis=1, keepdims=True)


def backward_kernel(rows, *refs):
    (nbr_hbm, q_ref, k_ref, v_ref, near_ref, far_ref, panel_ref, go_ref, attn_ref, p_hbm) = refs[
        :10
    ]
    (dq_ref, own_ref, to_near, to_far) = refs[10:14]
    (nbr_ref, ext_k, ext_v, sum_k, sum_v, p_ref, nbr_sem, p_sems) = refs[14:]
    tok, width = q_ref.shape
    blocks = tok // BLK
    fetch = pltpu.make_async_copy(nbr_hbm, nbr_ref, nbr_sem)
    fetch.start()
    loads = [
        pltpu.make_async_copy(p_hbm.at[b], p_ref.at[b], p_sems.at[b]) for b in range(blocks)
    ]
    for load in loads:
        load.start()
    odd = lax.axis_index("pix") & 1
    extend(ext_k, ext_v, k_ref, v_ref, near_ref, far_ref)
    panel_k, panel_v = panel_parts(panel_ref, rows)
    masks = head_masks(width, BLK)
    sum_k[...] = jnp.zeros_like(sum_k)
    sum_v[...] = jnp.zeros_like(sum_v)
    heads = len(masks)
    fetch.wait()
    for b in range(blocks):
        span = slice(b * BLK, (b + 1) * BLK)
        starts = picks(nbr_ref, b, blocks)
        q_tall = stacked(q_ref[span], masks)
        g_tall = stacked(go_ref[span], masks)
        dterm = row_terms(g_tall, attn_ref[span], heads)
        slope = mm_t(g_tall, gathered(ext_v, starts, panel_v))
        loads[b].wait()
        weights = p_ref[b]
        ds = (weights.astype(F32) * (slope - dterm)).astype(BF)
        dq = unstacked(mm(ds, gathered(ext_k, starts, panel_k)), masks)
        dq_ref[span] = (SCALE * dq).astype(BF)
        dk = SCALE * t_mm(ds[:, : NBR * BLK], q_tall)
        dv = t_mm(weights[:, : NBR * BLK], g_tall)
        for n in range(NBR):
            place = pl.ds(starts[n], BLK)
            sum_k[place, :] += dk[n * BLK : (n + 1) * BLK]
            sum_v[place, :] += dv[n * BLK : (n + 1) * BLK]
    own_ref[0:tok] = sum_k[RIM : RIM + tok]
    own_ref[tok:] = sum_v[RIM : RIM + tok]
    near = pl.ds(pl.multiple_of((1 - odd) * (tok + RIM), RIM), RIM)
    far = pl.ds(pl.multiple_of(odd * (tok + RIM), RIM), RIM)
    to_near[0:RIM] = sum_k[near, :].astype(BF)
    to_near[RIM:] = sum_v[near, :].astype(BF)
    to_far[0:RIM] = sum_k[far, :]
    to_far[RIM:] = sum_v[far, :]


def round_kernel(wide_ref, after_ref, out_ref):
    out_ref[...] = wide_ref[...].astype(BF)


def finish_kernel(
    own_ref, near_ref, far_ref, coarse_ref, pool_ref, gk_ref, gv_ref, ck_ref, cv_ref, acc_ref
):
    tok, width = gk_ref.shape
    rows = ck_ref.shape[0]
    odd = lax.axis_index("pix") & 1
    member = membership(pool_ref, rows).astype(F32)
    counts = jnp.sum(member, axis=1, keepdims=True)
    member = member.astype(BF)
    ck_ref[...] = coarse_ref[0:rows]
    cv_ref[...] = coarse_ref[rows:]
    member = jnp.concatenate([member, member], 0)
    near = pl.ds(pl.multiple_of((1 - odd) * (tok - RIM), RIM), RIM)
    far = pl.ds(pl.multiple_of(odd * (tok - RIM), RIM), RIM)
    for which, out in ((0, gk_ref), (1, gv_ref)):
        per_row = coarse_ref[which * rows : (which + 1) * rows] / counts
        high = per_row.astype(BF)
        low = (per_row - high.astype(F32)).astype(BF)
        pooled = t_mm(member, jnp.concatenate([high, low], 0))
        acc_ref[...] = own_ref[which * tok : (which + 1) * tok] + pooled
        half = slice(which * RIM, (which + 1) * RIM)
        acc_ref[near, :] += near_ref[half].astype(F32)
        acc_ref[far, :] += far_ref[half].astype(F32)
        out[...] = acc_ref[...].astype(BF)


def gw_kernel(levels, factor, *refs):
    out_ref = refs[-1]
    me = lax.axis_index("pix")
    chunk = out_ref.shape[0] >> levels
    mine = reversed_bits(me, levels)
    for slot, ref in enumerate(refs[:-1]):
        place = pl.ds(pl.multiple_of((slot ^ mine) * chunk, chunk), chunk)
        out_ref[place, :] = ref[...].astype(F32) * factor


def on_device(
    queries,
    keys,
    values,
    coarse_keys,
    coarse_values,
    neighbors,
    pool_map,
    coarse_mask,
    w_out,
    grad_mixed,
):
    tok, width = queries.shape
    rows = coarse_keys.shape[0]
    pix = lax.axis_size("pix")
    head = lax.axis_size("head")
    blocks = tok // BLK
    coarse = pix * rows
    d_model = head * width
    bits = bit_list(pix)
    head_bits = bit_list(head)
    levels = min(2, len(bits))
    heads = width // HDIM
    pool_row = pool_map.reshape(1, tok)
    q_in, gm_in, w_in, mask_in = queries, grad_mixed, w_out, coarse_mask
    keys_hbm, values_hbm, ck_hbm, cv_hbm, pool_hbm, nbr_hbm = [
        pltpu.with_memory_space_constraint(x, pltpu.HBM)
        for x in (
            keys,
            values,
            coarse_keys,
            coarse_values,
            pool_row,
            neighbors,
        )
    ]
    across = head
    slots = 1 << levels
    held = (pix // slots + across - 1) // across * 2 * rows
    chunk = width // slots
    segment = chunk + held

    k_own, v_own, panel, pool_own = call(
        prep_kernel,
        [((tok, width), BF), ((tok, width), BF), ((2 * rows, width), BF), ((1, tok), jnp.int32)],
        [HBM] * 5,
        scratch=[
            pltpu.VMEM((rows, width), BF),
            pltpu.VMEM((rows, width), BF),
            pltpu.SemaphoreType.DMA((5,)),
        ],
    )(keys_hbm, values_hbm, ck_hbm, cv_hbm, pool_hbm)
    grad_early, panel = lax.optimization_barrier((grad_mixed, panel))
    panel = gather_bits(panel, bits[:1])
    send_near, send_far = call(
        rim_kernel,
        [((2 * RIM, width), BF), ((2 * RIM, width), BF)],
        [VMEM] * 3,
        flops=3_000_000_000,
        bytes_accessed=4_000_000,
    )(k_own, v_own, panel)
    near = exchange(send_near, near_pairs(pix))
    late = (q_in, gm_in, w_in, mask_in)
    first = True
    for at in range(1, len(bits), 2):
        parts = gather_parts(panel, bits[at : at + 2])
        if first and len(parts) > 1:
            parts[1], send_far, *late = lax.optimization_barrier((parts[1], send_far, *late))
            first = False
        panel = jnp.concatenate(parts, 0)
    far = exchange(send_far, far_pairs(pix))
    q_own, gm_own, w_own, mask_own = call(
        load_kernel,
        [
            ((tok, width), BF),
            ((tok, width), BF),
            ((width, d_model), BF),
            (coarse_mask.shape, jnp.int32),
        ],
        [HBM] * 4,
        scratch=[pltpu.SemaphoreType.DMA((4,))],
        bytes_accessed=0,
    )(*[pltpu.with_memory_space_constraint(x, pltpu.HBM) for x in late])

    order = [grad_early]
    index = [0]
    for bit in reversed(head_bits):
        if len(order) > 1:
            *order, near = lax.optimization_barrier((*order, near))
        order = order + [swap(piece, "head", bit) for piece in order]
        index = index + [i ^ bit for i in index]
    grads = [order[index.index(j)] for j in range(1, head)]
    (grad_attn,) = call(
        grad_kernel,
        [((tok, width), BF)],
        [VMEM] * (1 + head),
        flops=0,
        bytes_accessed=0,
    )(w_own, gm_own, *grads)

    keys_each = NBR * BLK + coarse
    tall = heads * BLK
    product = 2 * tall * keys_each * width
    attn, weights, mix_keep, mix_send, gw_keep, gw_send = call(
        functools.partial(forward_kernel, rows, levels),
        [
            ((tok, width), BF),
            ((blocks, tall, keys_each), BF),
            ((head // 2 * tok, width), BF),
            ((head // 2 * tok, width), BF),
            ((slots // 2 * segment, d_model), BF),
            ((slots // 2 * segment, d_model), BF),
        ],
        [HBM] + [VMEM] * (9 + head),
        out_specs=[VMEM, HBM] + [VMEM] * 4,
        scratch=[
            pltpu.SMEM(neighbors.shape, jnp.int32),
            pltpu.VMEM((tok + 2 * RIM, width), BF),
            pltpu.VMEM((tok + 2 * RIM, width), BF),
            pltpu.VMEM((width, d_model), BF),
            pltpu.VMEM((blocks, tall, keys_each), BF),
            pltpu.SemaphoreType.DMA,
            pltpu.SemaphoreType.DMA((blocks,)),
        ],
        flops=2 * blocks * product + 4 * tok * width * d_model,
        bytes_accessed=10_000_000,
    )(
        nbr_hbm, mask_own, q_own, k_own, v_own, near, far, panel, w_own, grad_attn, gm_own, *grads
    )

    grad_queries, own, to_near, to_far = call(
        functools.partial(backward_kernel, rows),
        [
            ((tok, width), BF),
            ((2 * tok, width), F32),
            ((2 * RIM, width), BF),
            ((2 * RIM, width), F32),
        ],
        [HBM] + [VMEM] * 8 + [HBM],
        scratch=[
            pltpu.SMEM(neighbors.shape, jnp.int32),
            pltpu.VMEM((tok + 2 * RIM, width), BF),
            pltpu.VMEM((tok + 2 * RIM, width), BF),
            pltpu.VMEM((tok + 2 * RIM, width), F32),
            pltpu.VMEM((tok + 2 * RIM, width), F32),
            pltpu.VMEM((blocks, tall, keys_each), BF),
            pltpu.SemaphoreType.DMA,
            pltpu.SemaphoreType.DMA((blocks,)),
        ],
        flops=4 * blocks * product,
        bytes_accessed=10_000_000,
    )(nbr_hbm, q_own, k_own, v_own, near, far, panel, grad_attn, attn, pltpu.with_memory_space_constraint(weights, pltpu.HBM))

    kept, sent = gw_keep, gw_send
    for level in range(levels):
        got = swap(sent, "pix", bits[level])
        if level == 0:
            got, to_near, to_far = lax.optimization_barrier((got, to_near, to_far))
        total = kept.astype(F32) + got.astype(F32)
        half = total.shape[0] // 2
        if level + 1 < levels:
            kept, sent = total[:half], total[half:].astype(BF)
            sent, to_near = lax.optimization_barrier((sent, to_near))
    whole = total
    sent = lax.optimization_barrier(whole.astype(BF))
    (to_far,) = call(
        round_kernel,
        [((2 * RIM, width), BF)],
        [VMEM] * 2,
        flops=3_000_000_000,
        bytes_accessed=4_000_000,
    )(to_far, sent)
    cells = cut(whole[chunk:], 2 * rows, width, pix // slots)
    part = whole[:chunk]
    for bit in bits[levels:]:
        got = swap(sent, "pix", bit).astype(F32)
        part = part + got[:chunk]
        other = cut(got[chunk:], 2 * rows, width, len(cells))
        cells = [cells[t] + other[t ^ 1] for t in range(0, len(cells), 2)]
        if len(cells) > 1:
            empty = [jnp.zeros_like(cells[0])] * (-len(cells) % across)
            full = cells + empty
            lines = [
                jnp.concatenate(full[t : t + across], 1) for t in range(0, len(full), across)
            ]
            sent = jnp.concatenate([part] + lines, 0).astype(BF)
    coarse_grads = cells[0]
    part = part.astype(BF)
    gathered_parts = [part]
    for bit in reversed(bits[:levels]):
        gathered_parts = gathered_parts + [swap(p, "pix", bit) for p in gathered_parts]
        if len(gathered_parts) == 2:
            gathered_parts[1], coarse_grads = lax.optimization_barrier(
                (gathered_parts[1], coarse_grads)
            )
    (grad_w_out,) = call(
        functools.partial(gw_kernel, levels, (tok * pix) ** (-0.5)),
        [((width, d_model), F32)],
        [VMEM] * slots,
        flops=0,
        bytes_accessed=6 * width * d_model,
    )(*gathered_parts)

    kept, sent = mix_keep, mix_send
    for bit in head_bits:
        total = kept.astype(F32) + swap(sent, "head", bit).astype(F32)
        if kept.shape[0] > tok:
            half = kept.shape[0] // 2
            kept, sent = total[:half], total[half:].astype(BF)
    mixed = total.astype(BF)

    got_near = exchange(to_near, near_pairs(pix))
    got_far = exchange(to_far, far_pairs(pix))
    grad_keys, grad_values, grad_ck, grad_cv = call(
        finish_kernel,
        [((tok, width), BF), ((tok, width), BF), ((rows, width), F32), ((rows, width), F32)],
        [VMEM] * 5,
        scratch=[pltpu.VMEM((tok, width), F32)],
        flops=3_000_000_000,
        bytes_accessed=16 * tok * width,
    )(own, got_near, got_far, coarse_grads, pool_own)
    return (mixed, grad_queries, grad_keys, grad_values, grad_ck, grad_cv, grad_w_out)


def solution(mesh):
    in_specs = (
        P("pix", "head"),
        P("pix", "head"),
        P("pix", "head"),
        P("pix", "head"),
        P("pix", "head"),
        P("pix", None),
        P("pix"),
        P("pix", None),
        P("head", None),
        P("pix", "head"),
    )
    out_specs = (
        P("pix", "head"),
        P("pix", "head"),
        P("pix", "head"),
        P("pix", "head"),
        P("pix", "head"),
        P("pix", "head"),
        P("head", None),
    )
    return jax.shard_map(
        on_device, mesh=mesh, in_specs=in_specs, out_specs=out_specs, check_vma=False
    )
```

```python
import functools
import math

import jax
import jax.numpy as jnp
from jax import lax
from jax.experimental import pallas as pl
from jax.experimental.pallas import tpu as pltpu
from jax.sharding import PartitionSpec as P

HDIM = 64
BLK = 128
NBR = 4
HB = 2
CBLK = 8
RIM = HB * BLK
SCALE = HDIM ** (-0.5)
LOG2E = math.log2(math.e)
BF = jnp.bfloat16
F32 = jnp.float32
VMEM = pl.BlockSpec(memory_space=pltpu.VMEM)
HBM = pl.BlockSpec(memory_space=pltpu.HBM)


def mm(a, b):
    return jnp.dot(a, b, preferred_element_type=F32)


def mm_t(a, b):
    return lax.dot_general(a, b, (((1,), (1,)), ((), ())), preferred_element_type=F32)


def t_mm(a, b):
    return lax.dot_general(a, b, (((0,), (0,)), ((), ())), preferred_element_type=F32)


def bit_list(count):
    return [1 << i for i in range(count.bit_length() - 1)]


def swap(value, axis, bit):
    return lax.ppermute(value, axis, [(i, i ^ bit) for i in range(lax.axis_size(axis))])


def exchange(value, pairs):
    return lax.ppermute(value, "pix", pairs + [(b, a) for a, b in pairs])


def near_pairs(count):
    return [(i, i + 1) for i in range(0, count, 2)]


def far_pairs(count):
    return [(i, i + 1) for i in range(1, count - 1, 2)]


def gather_parts(value, bits):
    offsets = [0]
    for bit in bits:
        offsets = offsets + [o + bit for o in offsets]
    return [value if o == 0 else swap(value, "pix", o) for o in offsets]


def gather_bits(value, bits):
    return jnp.concatenate(gather_parts(value, bits), 0)


def cut(lines, height, width, count):
    across = lines.shape[1] // width
    cells = []
    for t in range(count):
        top, left = t // across * height, t % across * width
        cells.append(lines[top : top + height, left : left + width])
    return cells


def call(body, outs, specs, out_specs=None, scratch=(), flops=0, bytes_accessed=0):
    return pl.pallas_call(
        body,
        out_shape=[jax.ShapeDtypeStruct(s, t) for s, t in outs],
        in_specs=list(specs),
        out_specs=[VMEM] * len(outs) if out_specs is None else list(out_specs),
        scratch_shapes=list(scratch),
        compiler_params=pltpu.CompilerParams(vmem_limit_bytes=24 * 1024 * 1024),
        cost_estimate=pl.CostEstimate(
            flops=flops, bytes_accessed=bytes_accessed, transcendentals=0
        ),
    )


def membership(pool_ref, rows):
    me = lax.axis_index("pix")
    local = pool_ref[...] - me * rows
    count = pool_ref.shape[1]
    return local == lax.broadcasted_iota(jnp.int32, (rows, count), 0)


def prep_kernel(
    k_hbm, v_hbm, ck_hbm, cv_hbm, pool_hbm,
    k_ref, v_ref, panel_ref, pool_ref,
    ck_ref, cv_ref, sems,
):
    pairs = [
        (pool_hbm, pool_ref),
        (k_hbm, k_ref),
        (v_hbm, v_ref),
        (ck_hbm, ck_ref),
        (cv_hbm, cv_ref),
    ]
    copies = [pltpu.make_async_copy(x, y, sems.at[i]) for i, (x, y) in enumerate(pairs)]
    for copy in copies:
        copy.start()
    for copy in copies:
        copy.wait()
    member = membership(pool_ref, ck_ref.shape[0]).astype(F32)
    counts = jnp.sum(member, axis=1, keepdims=True)
    member = member.astype(BF)
    panel_k = mm(member, k_ref[...]) / counts + ck_ref[...].astype(F32)
    panel_v = mm(member, v_ref[...]) / counts + cv_ref[...].astype(F32)
    panel_ref[...] = jnp.concatenate([panel_k, panel_v], 0).astype(BF)


def rim_kernel(k_ref, v_ref, panel_ref, near_ref, far_ref):
    tok = k_ref.shape[0]
    odd = lax.axis_index("pix") & 1
    near = pl.ds(pl.multiple_of((1 - odd) * (tok - RIM), RIM), RIM)
    far = pl.ds(pl.multiple_of(odd * (tok - RIM), RIM), RIM)
    near_ref[0:RIM] = k_ref[near, :]
    near_ref[RIM:] = v_ref[near, :]
    far_ref[0:RIM] = k_ref[far, :]
    far_ref[RIM:] = v_ref[far, :]


def load_kernel(*refs):
    count = len(refs) // 2
    sems = refs[-1]
    copies = [
        pltpu.make_async_copy(refs[i], refs[count + i], sems.at[i]) for i in range(count)
    ]
    for copy in copies:
        copy.start()
    for copy in copies:
        copy.wait()


def grad_kernel(w_ref, *refs):
    pieces, go_ref = refs[:-1], refs[-1]
    me = lax.axis_index("head")
    width = w_ref.shape[0]
    total = None
    for j, ref in enumerate(pieces):
        w = w_ref[:, pl.ds(pl.multiple_of((me ^ j) * width, width), width)]
        part = mm_t(ref[...], w)
        total = part if total is None else total + part
    go_ref[...] = total.astype(BF)


def head_masks(width, rows):
    lane = lax.broadcasted_iota(jnp.int32, (rows, width), 1)
    return [(lane >= h * HDIM) & (lane < (h + 1) * HDIM) for h in range(width // HDIM)]


def stacked(block, masks):
    zero = jnp.zeros_like(block)
    return jnp.concatenate([jnp.where(m, block, zero) for m in masks], 0)


def unstacked(tall, masks):
    rows = tall.shape[0] // len(masks)
    out = tall[0:rows]
    for h in range(1, len(masks)):
        out = jnp.where(masks[h], tall[h * rows : (h + 1) * rows], out)
    return out


def extend(ext_k, ext_v, k_ref, v_ref, near_ref, far_ref):
    tok = k_ref.shape[0]
    odd = lax.axis_index("pix") & 1
    ext_k[RIM : RIM + tok] = k_ref[...]
    ext_v[RIM : RIM + tok] = v_ref[...]
    near = pl.ds(pl.multiple_of((1 - odd) * (tok + RIM), RIM), RIM)
    far = pl.ds(pl.multiple_of(odd * (tok + RIM), RIM), RIM)
    ext_k[near, :] = near_ref[0:RIM]
    ext_v[near, :] = near_ref[RIM:]
    ext_k[far, :] = far_ref[0:RIM]
    ext_v[far, :] = far_ref[RIM:]


def panel_parts(panel_ref, rows):
    width = panel_ref.shape[1]
    slots = panel_ref.shape[0] // (2 * rows)
    both = panel_ref[...].astype(F32).reshape(slots, 2 * rows, width)
    keys = both[:, :rows].reshape(slots * rows, width).astype(BF)
    values = both[:, rows:].reshape(slots * rows, width).astype(BF)
    return keys, values


def picks(nbr_ref, block, blocks):
    me = lax.axis_index("pix")
    starts = []
    for n in range(NBR):
        index = nbr_ref[block, n] - me * blocks + HB
        starts.append(pl.multiple_of(index * BLK, BLK))
    return starts


def gathered(ext, starts, panel):
    return jnp.concatenate([ext[pl.ds(s, BLK), :] for s in starts] + [panel], 0)


def forward_kernel(rows, levels, *refs):
    (nbr_hbm, mask_ref, q_ref, k_ref, v_ref, near_ref, far_ref, panel_ref, w_ref, go_ref) = refs[
        :10
    ]
    outs = len(refs) - 12 - (1 << levels)
    pieces = refs[10:outs]
    (e_ref, q_all, g_all, d_all, ext_k, ext_v) = refs[outs : outs + 6]
    (mix_keep, mix_send) = refs[outs + 6 : outs + 8]
    segments = refs[outs + 8 : outs + 8 + (1 << levels)]
    (nbr_ref, attn_ref, gw_all, nbr_sem) = refs[outs + 8 + (1 << levels) :]
    tok, width = q_ref.shape
    blocks = tok // BLK
    fetch = pltpu.make_async_copy(nbr_hbm, nbr_ref, nbr_sem)
    fetch.start()
    me = lax.axis_index("pix")
    me_head = lax.axis_index("head")
    extend(ext_k, ext_v, k_ref, v_ref, near_ref, far_ref)
    panel_k, panel_v = panel_parts(panel_ref, rows)
    coarse = panel_k.shape[0]
    cols = mask_ref.shape[1]
    row = lax.broadcasted_iota(jnp.int32, (cols, coarse), 1)
    owner_row = ((row // rows) ^ me) * rows + row % rows
    pick = (owner_row // CBLK) == lax.broadcasted_iota(jnp.int32, (cols, coarse), 0)
    allowed = mm((mask_ref[...] > 0).astype(BF), pick.astype(BF))
    masks = head_masks(width, BLK)
    heads = len(masks)
    coarse_k = jnp.zeros((coarse, width), F32)
    coarse_v = jnp.zeros((coarse, width), F32)
    fetch.wait()
    for b in range(blocks):
        span = slice(b * BLK, (b + 1) * BLK)
        starts = picks(nbr_ref, b, blocks)
        q_tall = stacked(q_ref[span], masks)
        q_all[b] = q_tall
        scores = mm_t(q_tall, gathered(ext_k, starts, panel_k)) * (SCALE * LOG2E)
        fine = scores[:, : NBR * BLK]
        lo = jnp.where(allowed[b : b + 1] > 0.5, scores[:, NBR * BLK :], -jnp.inf)
        top = jnp.maximum(
            jnp.max(fine, axis=1, keepdims=True), jnp.max(lo, axis=1, keepdims=True)
        )
        fine = jnp.exp2(fine - top)
        lo = jnp.exp2(lo - top)
        total = jnp.sum(fine, axis=1, keepdims=True) + jnp.sum(lo, axis=1, keepdims=True)
        scale = 1.0 / total
        coarse_e = lo.astype(BF)
        weights = jnp.concatenate([fine.astype(BF), coarse_e], 1)
        e_ref[b] = weights
        out = mm(weights, gathered(ext_v, starts, panel_v)) * scale
        attn = unstacked(out, masks).astype(BF)
        attn_ref[span] = attn
        g_tall = stacked(go_ref[span], masks).astype(F32) * scale
        dterm = jnp.sum(
            g_tall * jnp.concatenate([attn.astype(F32)] * heads, 0), axis=1, keepdims=True
        )
        g_tall = g_tall.astype(BF)
        g_all[b] = g_tall
        d_all[b] = dterm
    tall_g = g_all[...].reshape(blocks * heads * BLK, width)
    tall_q = q_all[...].reshape(blocks * heads * BLK, width)
    tall_d = d_all[...].reshape(blocks * heads * BLK, 1)
    tall_e = e_ref[:, :, NBR * BLK :].reshape(blocks * heads * BLK, coarse)
    coarse_ds = tall_e.astype(F32) * (mm_t(tall_g, panel_v) - tall_d)
    coarse_k = SCALE * t_mm(coarse_ds.astype(BF), tall_q)
    coarse_v = t_mm(tall_e, tall_g)
    attn = attn_ref[...]
    chunk = width >> levels
    mine = me & ((1 << levels) - 1)
    for j, piece in enumerate(pieces):
        part = t_mm(attn, piece[...]).astype(BF)
        lanes = pl.ds(pl.multiple_of((me_head ^ j) * width, width), width)
        for c in range(1 << levels):
            place = pl.ds(pl.multiple_of((c ^ mine) * chunk, chunk), chunk)
            gw_all[place, lanes] = part[c * chunk : (c + 1) * chunk]
    for j, piece in enumerate(pieces):
        lanes = pl.ds(pl.multiple_of((me_head ^ j) * width, width), width)
        part = mm(attn, w_ref[:, lanes]).astype(BF)
        target = mix_send if j & 1 else mix_keep
        target[(j >> 1) * tok : ((j >> 1) + 1) * tok] = part
    across = gw_all.shape[1] // width
    for m, target in enumerate(segments):
        target[:chunk] = gw_all[m * chunk : (m + 1) * chunk]
        if (coarse // rows) >> levels < across:
            target[chunk:] = jnp.zeros_like(target[chunk:])
    for j in range(coarse // rows):
        t = j >> levels
        base = chunk + (t // across) * 2 * rows
        lanes = slice((t % across) * width, (t % across + 1) * width)
        both = [coarse_k[j * rows : (j + 1) * rows], coarse_v[j * rows : (j + 1) * rows]]
        target = segments[j & ((1 << levels) - 1)]
        target[base : base + 2 * rows, lanes] = jnp.concatenate(both, 0).astype(BF)


def backward_kernel(rows, *refs):
    (nbr_hbm, panel_ref, e_ref, q_all, g_all, d_all, ext_k, ext_v) = refs[:8]
    (dq_ref, own_ref, to_near, to_far) = refs[8:12]
    (nbr_ref, sum_k, sum_v, nbr_sem) = refs[12:]
    tok, width = dq_ref.shape
    blocks = tok // BLK
    fetch = pltpu.make_async_copy(nbr_hbm, nbr_ref, nbr_sem)
    fetch.start()
    odd = lax.axis_index("pix") & 1
    panel_k, panel_v = panel_parts(panel_ref, rows)
    masks = head_masks(width, BLK)
    sum_k[...] = jnp.zeros_like(sum_k)
    sum_v[...] = jnp.zeros_like(sum_v)
    fetch.wait()
    for b in range(blocks):
        span = slice(b * BLK, (b + 1) * BLK)
        starts = picks(nbr_ref, b, blocks)
        g_tall = g_all[b]
        weights = e_ref[b]
        dv = t_mm(weights[:, : NBR * BLK], g_tall)
        slope = mm_t(g_tall, gathered(ext_v, starts, panel_v))
        ds = (weights.astype(F32) * (slope - d_all[b])).astype(BF)
        dq = unstacked(mm(ds, gathered(ext_k, starts, panel_k)), masks)
        dq_ref[span] = (SCALE * dq).astype(BF)
        dk = t_mm(ds[:, : NBR * BLK], q_all[b])
        for n in range(NBR):
            place = pl.ds(starts[n], BLK)
            sum_k[place, :] += dk[n * BLK : (n + 1) * BLK]
            sum_v[place, :] += dv[n * BLK : (n + 1) * BLK]
    own_ref[0:tok] = SCALE * sum_k[RIM : RIM + tok]
    own_ref[tok:] = sum_v[RIM : RIM + tok]
    near = pl.ds(pl.multiple_of((1 - odd) * (tok + RIM), RIM), RIM)
    far = pl.ds(pl.multiple_of(odd * (tok + RIM), RIM), RIM)
    to_near[0:RIM] = (SCALE * sum_k[near, :]).astype(BF)
    to_near[RIM:] = sum_v[near, :].astype(BF)
    to_far[0:RIM] = SCALE * sum_k[far, :]
    to_far[RIM:] = sum_v[far, :]


def round_kernel(wide_ref, after_ref, out_ref):
    out_ref[...] = wide_ref[...].astype(BF)


def finish_kernel(
    own_ref, near_ref, far_ref, coarse_ref, pool_ref, gk_ref, gv_ref, ck_ref, cv_ref, acc_ref
):
    tok, width = gk_ref.shape
    rows = ck_ref.shape[0]
    odd = lax.axis_index("pix") & 1
    member = membership(pool_ref, rows).astype(F32)
    counts = jnp.sum(member, axis=1, keepdims=True)
    member = member.astype(BF)
    ck_ref[...] = coarse_ref[0:rows]
    cv_ref[...] = coarse_ref[rows:]
    member = jnp.concatenate([member, member], 0)
    near = pl.ds(pl.multiple_of((1 - odd) * (tok - RIM), RIM), RIM)
    far = pl.ds(pl.multiple_of(odd * (tok - RIM), RIM), RIM)
    for which, out in ((0, gk_ref), (1, gv_ref)):
        per_row = coarse_ref[which * rows : (which + 1) * rows] / counts
        high = per_row.astype(BF)
        low = (per_row - high.astype(F32)).astype(BF)
        pooled = t_mm(member, jnp.concatenate([high, low], 0))
        acc_ref[...] = own_ref[which * tok : (which + 1) * tok] + pooled
        half = slice(which * RIM, (which + 1) * RIM)
        acc_ref[near, :] += near_ref[half].astype(F32)
        acc_ref[far, :] += far_ref[half].astype(F32)
        out[...] = acc_ref[...].astype(BF)


def gw_kernel(levels, factor, *refs):
    out_ref = refs[-1]
    me = lax.axis_index("pix")
    chunk = out_ref.shape[0] >> levels
    mine = me & ((1 << levels) - 1)
    for slot, ref in enumerate(refs[:-1]):
        place = pl.ds(pl.multiple_of((slot ^ mine) * chunk, chunk), chunk)
        out_ref[place, :] = ref[...].astype(F32) * factor


def run_forward(rows, coarse, levels, segment, args, pieces):
    tok, width = args[2].shape
    d_model = args[8].shape[1]
    head = len(pieces)
    blocks = tok // BLK
    keys_each = NBR * BLK + coarse
    tall = width // HDIM * BLK
    kept = [
        ((blocks, tall, keys_each), BF),
        ((blocks, tall, width), BF),
        ((blocks, tall, width), BF),
        ((blocks, tall, 1), F32),
        ((tok + 2 * RIM, width), BF),
        ((tok + 2 * RIM, width), BF),
    ]
    outs = call(
        functools.partial(forward_kernel, rows, levels),
        kept
        + [((head // 2 * tok, width), BF)] * 2
        + [((segment, d_model), BF)] * (1 << levels),
        [HBM] + [VMEM] * (9 + head),
        scratch=[
            pltpu.SMEM(args[0].shape, jnp.int32),
            pltpu.VMEM((tok, width), BF),
            pltpu.VMEM((width, d_model), BF),
            pltpu.SemaphoreType.DMA,
        ],
        flops=4 * blocks * tall * keys_each * width + 4 * tok * width * d_model,
        bytes_accessed=10_000_000,
    )(*args, *pieces)
    return outs[: len(kept)], outs[len(kept) :]


def run_backward(rows, neighbors, panel, saved):
    blocks, tall, width = saved[1].shape
    tok = blocks * BLK
    return call(
        functools.partial(backward_kernel, rows),
        [
            ((tok, width), BF),
            ((2 * tok, width), F32),
            ((2 * RIM, width), BF),
            ((2 * RIM, width), F32),
        ],
        [HBM] + [VMEM] * 7,
        scratch=[
            pltpu.SMEM(neighbors.shape, jnp.int32),
            pltpu.VMEM((tok + 2 * RIM, width), F32),
            pltpu.VMEM((tok + 2 * RIM, width), F32),
            pltpu.SemaphoreType.DMA,
        ],
        flops=8 * blocks * tall * saved[0].shape[2] * width,
        bytes_accessed=10_000_000,
    )(neighbors, panel, *saved)


def on_device(
    queries,
    keys,
    values,
    coarse_keys,
    coarse_values,
    neighbors,
    pool_map,
    coarse_mask,
    w_out,
    grad_mixed,
):
    tok, width = queries.shape
    rows = coarse_keys.shape[0]
    pix = lax.axis_size("pix")
    head = lax.axis_size("head")
    blocks = tok // BLK
    coarse = pix * rows
    d_model = head * width
    bits = bit_list(pix)
    head_bits = bit_list(head)
    levels = min(2, len(bits))
    pool_row = pool_map.reshape(1, tok)
    q_in, gm_in, w_in, mask_in = queries, grad_mixed, w_out, coarse_mask
    keys_hbm, values_hbm, ck_hbm, cv_hbm, pool_hbm, nbr_hbm = [
        pltpu.with_memory_space_constraint(x, pltpu.HBM)
        for x in (
            keys,
            values,
            coarse_keys,
            coarse_values,
            pool_row,
            neighbors,
        )
    ]
    across = head
    slots = 1 << levels
    held = (pix // slots + across - 1) // across * 2 * rows
    chunk = width // slots
    segment = chunk + held

    k_own, v_own, panel, pool_own = call(
        prep_kernel,
        [((tok, width), BF), ((tok, width), BF), ((2 * rows, width), BF), ((1, tok), jnp.int32)],
        [HBM] * 5,
        scratch=[
            pltpu.VMEM((rows, width), BF),
            pltpu.VMEM((rows, width), BF),
            pltpu.SemaphoreType.DMA((5,)),
        ],
    )(keys_hbm, values_hbm, ck_hbm, cv_hbm, pool_hbm)
    grad_early, panel = lax.optimization_barrier((grad_mixed, panel))
    panel = gather_bits(panel, bits[:1])
    send_near, send_far = call(
        rim_kernel,
        [((2 * RIM, width), BF), ((2 * RIM, width), BF)],
        [VMEM] * 3,
        flops=3_000_000_000,
        bytes_accessed=4_000_000,
    )(k_own, v_own, panel)
    near = exchange(send_near, near_pairs(pix))
    late = (q_in, gm_in, w_in, mask_in)
    first = True
    for at in range(1, len(bits), 2):
        parts = gather_parts(panel, bits[at : at + 2])
        if first and len(parts) > 1:
            parts[1], send_far, *late = lax.optimization_barrier((parts[1], send_far, *late))
            first = False
        panel = jnp.concatenate(parts, 0)
    far = exchange(send_far, far_pairs(pix))
    q_own, gm_own, w_own, mask_own = call(
        load_kernel,
        [
            ((tok, width), BF),
            ((tok, width), BF),
            ((width, d_model), BF),
            (coarse_mask.shape, jnp.int32),
        ],
        [HBM] * 4,
        scratch=[pltpu.SemaphoreType.DMA((4,))],
        bytes_accessed=0,
    )(*[pltpu.with_memory_space_constraint(x, pltpu.HBM) for x in late])

    order = [grad_early]
    index = [0]
    for bit in reversed(head_bits):
        if len(order) > 1:
            order[0] = gm_own
            *order, near = lax.optimization_barrier((*order, near))
        order = order + [swap(piece, "head", bit) for piece in order]
        index = index + [i ^ bit for i in index]
    grads = [order[index.index(j)] for j in range(1, head)]
    (grad_attn,) = call(
        grad_kernel,
        [((tok, width), BF)],
        [VMEM] * (1 + head),
        flops=0,
        bytes_accessed=0,
    )(w_own, gm_own, *grads)

    saved, (mix_keep, mix_send, *segments) = run_forward(
        rows,
        coarse,
        levels,
        segment,
        (nbr_hbm, mask_own, q_own, k_own, v_own, near, far, panel, w_own, grad_attn),
        (gm_own, *grads),
    )
    grad_queries, own, to_near, to_far = run_backward(rows, nbr_hbm, panel, saved)

    got = [swap(segments[m], "pix", m) for m in range(1, slots)]
    *got, to_near = lax.optimization_barrier((*got, to_near))
    total = segments[0].astype(F32)
    for piece in got:
        total = total + piece.astype(F32)
    whole = total
    sent = lax.optimization_barrier(whole.astype(BF))
    (to_far,) = call(
        round_kernel,
        [((2 * RIM, width), BF)],
        [VMEM] * 2,
        flops=3_000_000_000,
        bytes_accessed=4_000_000,
    )(to_far, sent)
    cells = cut(whole[chunk:], 2 * rows, width, pix // slots)
    part = whole[:chunk]
    for bit in bits[levels:]:
        got = swap(sent, "pix", bit).astype(F32)
        part = part + got[:chunk]
        other = cut(got[chunk:], 2 * rows, width, len(cells))
        cells = [cells[t] + other[t ^ 1] for t in range(0, len(cells), 2)]
        if len(cells) > 1:
            empty = [jnp.zeros_like(cells[0])] * (-len(cells) % across)
            full = cells + empty
            lines = [
                jnp.concatenate(full[t : t + across], 1) for t in range(0, len(full), across)
            ]
            sent = jnp.concatenate([part] + lines, 0).astype(BF)
    coarse_grads = cells[0]
    part = part.astype(BF)
    part, coarse_grads = lax.optimization_barrier((part, coarse_grads))
    gathered_parts = [part] + [swap(part, "pix", m) for m in range(1, slots)]
    (grad_w_out,) = call(
        functools.partial(gw_kernel, levels, (tok * pix) ** (-0.5)),
        [((width, d_model), F32)],
        [VMEM] * slots,
        flops=0,
        bytes_accessed=6 * width * d_model,
    )(*gathered_parts)

    kept, sent = mix_keep, mix_send
    for bit in head_bits:
        total = kept.astype(F32) + swap(sent, "head", bit).astype(F32)
        if kept.shape[0] > tok:
            half = kept.shape[0] // 2
            kept, sent = total[:half], total[half:].astype(BF)
    mixed = total.astype(BF)

    got_near = exchange(to_near, near_pairs(pix))
    got_far = exchange(to_far, far_pairs(pix))
    grad_keys, grad_values, grad_ck, grad_cv = call(
        finish_kernel,
        [((tok, width), BF), ((tok, width), BF), ((rows, width), F32), ((rows, width), F32)],
        [VMEM] * 5,
        scratch=[pltpu.VMEM((tok, width), F32)],
        flops=3_000_000_000,
        bytes_accessed=16 * tok * width,
    )(own, got_near, got_far, coarse_grads, pool_own)
    return (mixed, grad_queries, grad_keys, grad_values, grad_ck, grad_cv, grad_w_out)


def solution(mesh):
    in_specs = (
        P("pix", "head"),
        P("pix", "head"),
        P("pix", "head"),
        P("pix", "head"),
        P("pix", "head"),
        P("pix", None),
        P("pix"),
        P("pix", None),
        P("head", None),
        P("pix", "head"),
    )
    out_specs = (
        P("pix", "head"),
        P("pix", "head"),
        P("pix", "head"),
        P("pix", "head"),
        P("pix", "head"),
        P("pix", "head"),
        P("head", None),
    )
    return jax.shard_map(
        on_device, mesh=mesh, in_specs=in_specs, out_specs=out_specs, check_vma=False
    )
```

```python
import functools
import math

import jax
import jax.numpy as jnp
from jax import lax
from jax.experimental import pallas as pl
from jax.experimental.pallas import tpu as pltpu
from jax.sharding import PartitionSpec as P

HDIM = 64
BLK = 128
NBR = 4
HB = 2
CBLK = 8
RIM = HB * BLK
SCALE = HDIM ** (-0.5)
LOG2E = math.log2(math.e)
BF = jnp.bfloat16
F32 = jnp.float32
VMEM = pl.BlockSpec(memory_space=pltpu.VMEM)
HBM = pl.BlockSpec(memory_space=pltpu.HBM)


def mm(a, b):
    return jnp.dot(a, b, preferred_element_type=F32)


def mm_t(a, b):
    return lax.dot_general(a, b, (((1,), (1,)), ((), ())), preferred_element_type=F32)


def t_mm(a, b):
    return lax.dot_general(a, b, (((0,), (0,)), ((), ())), preferred_element_type=F32)


def bit_list(count):
    return [1 << i for i in range(count.bit_length() - 1)]


def swap(value, axis, bit):
    return lax.ppermute(value, axis, [(i, i ^ bit) for i in range(lax.axis_size(axis))])


def exchange(value, pairs):
    return lax.ppermute(value, "pix", pairs + [(b, a) for a, b in pairs])


def near_pairs(count):
    return [(i, i + 1) for i in range(0, count, 2)]


def far_pairs(count):
    return [(i, i + 1) for i in range(1, count - 1, 2)]


def gather_parts(value, bits):
    offsets = [0]
    for bit in bits:
        offsets = offsets + [o + bit for o in offsets]
    return [value if o == 0 else swap(value, "pix", o) for o in offsets]


def gather_bits(value, bits):
    return jnp.concatenate(gather_parts(value, bits), 0)


def cut(lines, height, width, count):
    across = lines.shape[1] // width
    cells = []
    for t in range(count):
        top, left = t // across * height, t % across * width
        cells.append(lines[top : top + height, left : left + width])
    return cells


def call(body, outs, specs, out_specs=None, scratch=(), flops=0, bytes_accessed=0):
    return pl.pallas_call(
        body,
        out_shape=[jax.ShapeDtypeStruct(s, t) for s, t in outs],
        in_specs=list(specs),
        out_specs=[VMEM] * len(outs) if out_specs is None else list(out_specs),
        scratch_shapes=list(scratch),
        compiler_params=pltpu.CompilerParams(vmem_limit_bytes=24 * 1024 * 1024),
        cost_estimate=pl.CostEstimate(
            flops=flops, bytes_accessed=bytes_accessed, transcendentals=0
        ),
    )


def membership(pool_ref, rows):
    me = lax.axis_index("pix")
    local = pool_ref[...] - me * rows
    count = pool_ref.shape[1]
    return local == lax.broadcasted_iota(jnp.int32, (rows, count), 0)


def prep_kernel(
    k_hbm, v_hbm, ck_hbm, cv_hbm, pool_hbm,
    k_ref, v_ref, panel_ref, pool_ref,
    ck_ref, cv_ref, sems,
):
    pairs = [
        (pool_hbm, pool_ref),
        (k_hbm, k_ref),
        (v_hbm, v_ref),
        (ck_hbm, ck_ref),
        (cv_hbm, cv_ref),
    ]
    copies = [pltpu.make_async_copy(x, y, sems.at[i]) for i, (x, y) in enumerate(pairs)]
    for copy in copies:
        copy.start()
    for copy in copies:
        copy.wait()
    member = membership(pool_ref, ck_ref.shape[0]).astype(F32)
    counts = jnp.sum(member, axis=1, keepdims=True)
    member = member.astype(BF)
    panel_k = mm(member, k_ref[...]) / counts + ck_ref[...].astype(F32)
    panel_v = mm(member, v_ref[...]) / counts + cv_ref[...].astype(F32)
    panel_ref[...] = jnp.concatenate([panel_k, panel_v], 0).astype(BF)


def rim_kernel(k_ref, v_ref, panel_ref, near_ref, far_ref):
    tok = k_ref.shape[0]
    odd = lax.axis_index("pix") & 1
    near = pl.ds(pl.multiple_of((1 - odd) * (tok - RIM), RIM), RIM)
    far = pl.ds(pl.multiple_of(odd * (tok - RIM), RIM), RIM)
    near_ref[0:RIM] = k_ref[near, :]
    near_ref[RIM:] = v_ref[near, :]
    far_ref[0:RIM] = k_ref[far, :]
    far_ref[RIM:] = v_ref[far, :]


def load_kernel(*refs):
    count = len(refs) // 2
    sems = refs[-1]
    copies = [
        pltpu.make_async_copy(refs[i], refs[count + i], sems.at[i]) for i in range(count)
    ]
    for copy in copies:
        copy.start()
    for copy in copies:
        copy.wait()


def grad_kernel(w_ref, *refs):
    pieces, go_ref = refs[:-1], refs[-1]
    me = lax.axis_index("head")
    width = w_ref.shape[0]
    total = None
    for j, ref in enumerate(pieces):
        w = w_ref[:, pl.ds(pl.multiple_of((me ^ j) * width, width), width)]
        part = mm_t(ref[...], w)
        total = part if total is None else total + part
    go_ref[...] = total.astype(BF)


def head_masks(width, rows):
    lane = lax.broadcasted_iota(jnp.int32, (rows, width), 1)
    return [(lane >= h * HDIM) & (lane < (h + 1) * HDIM) for h in range(width // HDIM)]


def stacked(block, masks):
    zero = jnp.zeros_like(block)
    return jnp.concatenate([jnp.where(m, block, zero) for m in masks], 0)


def unstacked(tall, masks):
    rows = tall.shape[0] // len(masks)
    out = tall[0:rows]
    for h in range(1, len(masks)):
        out = jnp.where(masks[h], tall[h * rows : (h + 1) * rows], out)
    return out


def extend(ext_k, ext_v, k_ref, v_ref, near_ref, far_ref):
    tok = k_ref.shape[0]
    odd = lax.axis_index("pix") & 1
    ext_k[RIM : RIM + tok] = k_ref[...]
    ext_v[RIM : RIM + tok] = v_ref[...]
    near = pl.ds(pl.multiple_of((1 - odd) * (tok + RIM), RIM), RIM)
    far = pl.ds(pl.multiple_of(odd * (tok + RIM), RIM), RIM)
    ext_k[near, :] = near_ref[0:RIM]
    ext_v[near, :] = near_ref[RIM:]
    ext_k[far, :] = far_ref[0:RIM]
    ext_v[far, :] = far_ref[RIM:]


def panel_parts(panel_ref, rows):
    width = panel_ref.shape[1]
    slots = panel_ref.shape[0] // (2 * rows)
    both = panel_ref[...].astype(F32).reshape(slots, 2 * rows, width)
    keys = both[:, :rows].reshape(slots * rows, width).astype(BF)
    values = both[:, rows:].reshape(slots * rows, width).astype(BF)
    return keys, values


def picks(nbr_ref, block, blocks):
    me = lax.axis_index("pix")
    starts = []
    for n in range(NBR):
        index = nbr_ref[block, n] - me * blocks + HB
        starts.append(pl.multiple_of(index * BLK, BLK))
    return starts


def gathered(ext, starts, panel):
    return jnp.concatenate([ext[pl.ds(s, BLK), :] for s in starts] + [panel], 0)


def forward_kernel(rows, levels, *refs):
    (nbr_hbm, mask_ref, q_ref, k_ref, v_ref, near_ref, far_ref, panel_ref, w_ref, go_ref) = refs[
        :10
    ]
    outs = len(refs) - 12 - (1 << levels)
    pieces = refs[10:outs]
    (e_ref, q_all, g_all, d_all, ext_k, ext_v) = refs[outs : outs + 6]
    (mix_keep, mix_send) = refs[outs + 6 : outs + 8]
    segments = refs[outs + 8 : outs + 8 + (1 << levels)]
    (nbr_ref, attn_ref, gw_all, nbr_sem) = refs[outs + 8 + (1 << levels) :]
    tok, width = q_ref.shape
    blocks = tok // BLK
    fetch = pltpu.make_async_copy(nbr_hbm, nbr_ref, nbr_sem)
    fetch.start()
    me = lax.axis_index("pix")
    me_head = lax.axis_index("head")
    extend(ext_k, ext_v, k_ref, v_ref, near_ref, far_ref)
    panel_k, panel_v = panel_parts(panel_ref, rows)
    coarse = panel_k.shape[0]
    cols = mask_ref.shape[1]
    row = lax.broadcasted_iota(jnp.int32, (cols, coarse), 1)
    owner_row = ((row // rows) ^ me) * rows + row % rows
    pick = (owner_row // CBLK) == lax.broadcasted_iota(jnp.int32, (cols, coarse), 0)
    allowed = mm((mask_ref[...] > 0).astype(BF), pick.astype(BF))
    masks = head_masks(width, BLK)
    heads = len(masks)
    coarse_k = jnp.zeros((coarse, width), F32)
    coarse_v = jnp.zeros((coarse, width), F32)
    fetch.wait()
    for b in range(blocks):
        span = slice(b * BLK, (b + 1) * BLK)
        starts = picks(nbr_ref, b, blocks)
        q_tall = stacked(q_ref[span], masks)
        q_all[b] = q_tall
        scores = mm_t(q_tall, gathered(ext_k, starts, panel_k)) * (SCALE * LOG2E)
        fine = scores[:, : NBR * BLK]
        lo = jnp.where(allowed[b : b + 1] > 0.5, scores[:, NBR * BLK :], -jnp.inf)
        top = jnp.maximum(
            jnp.max(fine, axis=1, keepdims=True), jnp.max(lo, axis=1, keepdims=True)
        )
        fine = jnp.exp2(fine - top)
        lo = jnp.exp2(lo - top)
        total = jnp.sum(fine, axis=1, keepdims=True) + jnp.sum(lo, axis=1, keepdims=True)
        scale = 1.0 / total
        coarse_e = lo.astype(BF)
        weights = jnp.concatenate([fine.astype(BF), coarse_e], 1)
        e_ref[b] = weights
        out = mm(weights, gathered(ext_v, starts, panel_v)) * scale
        attn = unstacked(out, masks).astype(BF)
        attn_ref[span] = attn
        g_tall = stacked(go_ref[span], masks).astype(F32) * scale
        dterm = jnp.sum(
            g_tall * jnp.concatenate([attn.astype(F32)] * heads, 0), axis=1, keepdims=True
        )
        g_tall = g_tall.astype(BF)
        g_all[b] = g_tall
        d_all[b] = dterm
    tall_g = g_all[...].reshape(blocks * heads * BLK, width)
    tall_q = q_all[...].reshape(blocks * heads * BLK, width)
    tall_d = d_all[...].reshape(blocks * heads * BLK, 1)
    tall_e = e_ref[:, :, NBR * BLK :].reshape(blocks * heads * BLK, coarse)
    coarse_ds = tall_e.astype(F32) * (mm_t(tall_g, panel_v) - tall_d)
    coarse_k = SCALE * t_mm(coarse_ds.astype(BF), tall_q)
    coarse_v = t_mm(tall_e, tall_g)
    attn = attn_ref[...]
    chunk = width >> levels
    mine = me & ((1 << levels) - 1)
    for j, piece in enumerate(pieces):
        part = t_mm(attn, piece[...]).astype(BF)
        lanes = pl.ds(pl.multiple_of((me_head ^ j) * width, width), width)
        for c in range(1 << levels):
            place = pl.ds(pl.multiple_of((c ^ mine) * chunk, chunk), chunk)
            gw_all[place, lanes] = part[c * chunk : (c + 1) * chunk]
    for j, piece in enumerate(pieces):
        lanes = pl.ds(pl.multiple_of((me_head ^ j) * width, width), width)
        part = mm(attn, w_ref[:, lanes]).astype(BF)
        target = mix_send if j & 1 else mix_keep
        target[(j >> 1) * tok : ((j >> 1) + 1) * tok] = part
    across = gw_all.shape[1] // (2 * width)
    for m, target in enumerate(segments):
        cells = []
        for j in range(m, coarse // rows, 1 << levels):
            span = slice(j * rows, (j + 1) * rows)
            cells.append(jnp.concatenate([coarse_k[span], coarse_v[span]], 1))
        cells = cells + [jnp.zeros_like(cells[0])] * (-len(cells) % across)
        lines = [
            jnp.concatenate(cells[t : t + across], 1) for t in range(0, len(cells), across)
        ]
        own = gw_all[m * chunk : (m + 1) * chunk].astype(F32)
        target[...] = jnp.concatenate([own] + lines, 0).astype(BF)


def backward_kernel(rows, *refs):
    (nbr_hbm, panel_ref, e_ref, q_all, g_all, d_all, ext_k, ext_v) = refs[:8]
    (dq_ref, own_ref, to_near, to_far) = refs[8:12]
    (nbr_ref, sum_k, sum_v, nbr_sem) = refs[12:]
    tok, width = dq_ref.shape
    blocks = tok // BLK
    fetch = pltpu.make_async_copy(nbr_hbm, nbr_ref, nbr_sem)
    fetch.start()
    odd = lax.axis_index("pix") & 1
    panel_k, panel_v = panel_parts(panel_ref, rows)
    masks = head_masks(width, BLK)
    sum_k[...] = jnp.zeros_like(sum_k)
    sum_v[...] = jnp.zeros_like(sum_v)
    fetch.wait()
    for b in range(blocks):
        span = slice(b * BLK, (b + 1) * BLK)
        starts = picks(nbr_ref, b, blocks)
        g_tall = g_all[b]
        weights = e_ref[b]
        dv = t_mm(weights[:, : NBR * BLK], g_tall)
        slope = mm_t(g_tall, gathered(ext_v, starts, panel_v))
        ds = (weights.astype(F32) * (slope - d_all[b])).astype(BF)
        dq = unstacked(mm(ds, gathered(ext_k, starts, panel_k)), masks)
        dq_ref[span] = (SCALE * dq).astype(BF)
        dk = t_mm(ds[:, : NBR * BLK], q_all[b])
        for n in range(NBR):
            place = pl.ds(starts[n], BLK)
            sum_k[place, :] += dk[n * BLK : (n + 1) * BLK]
            sum_v[place, :] += dv[n * BLK : (n + 1) * BLK]
    own_ref[0:tok] = SCALE * sum_k[RIM : RIM + tok]
    own_ref[tok:] = sum_v[RIM : RIM + tok]
    near = pl.ds(pl.multiple_of((1 - odd) * (tok + RIM), RIM), RIM)
    far = pl.ds(pl.multiple_of(odd * (tok + RIM), RIM), RIM)
    to_near[0:RIM] = (SCALE * sum_k[near, :]).astype(BF)
    to_near[RIM:] = sum_v[near, :].astype(BF)
    to_far[0:RIM] = SCALE * sum_k[far, :]
    to_far[RIM:] = sum_v[far, :]


def round_kernel(wide_ref, after_ref, out_ref):
    out_ref[...] = wide_ref[...].astype(BF)


def finish_kernel(
    own_ref, near_ref, far_ref, coarse_ref, pool_ref, gk_ref, gv_ref, ck_ref, cv_ref, acc_ref
):
    tok, width = gk_ref.shape
    rows = ck_ref.shape[0]
    odd = lax.axis_index("pix") & 1
    member = membership(pool_ref, rows).astype(F32)
    counts = jnp.sum(member, axis=1, keepdims=True)
    member = member.astype(BF)
    ck_ref[...] = coarse_ref[:, :width]
    cv_ref[...] = coarse_ref[:, width:]
    member = jnp.concatenate([member, member], 0)
    near = pl.ds(pl.multiple_of((1 - odd) * (tok - RIM), RIM), RIM)
    far = pl.ds(pl.multiple_of(odd * (tok - RIM), RIM), RIM)
    for which, out in ((0, gk_ref), (1, gv_ref)):
        per_row = coarse_ref[:, which * width : (which + 1) * width] / counts
        high = per_row.astype(BF)
        low = (per_row - high.astype(F32)).astype(BF)
        pooled = t_mm(member, jnp.concatenate([high, low], 0))
        acc_ref[...] = own_ref[which * tok : (which + 1) * tok] + pooled
        half = slice(which * RIM, (which + 1) * RIM)
        acc_ref[near, :] += near_ref[half].astype(F32)
        acc_ref[far, :] += far_ref[half].astype(F32)
        out[...] = acc_ref[...].astype(BF)


def gw_kernel(levels, factor, *refs):
    out_ref = refs[-1]
    me = lax.axis_index("pix")
    chunk = out_ref.shape[0] >> levels
    mine = me & ((1 << levels) - 1)
    for slot, ref in enumerate(refs[:-1]):
        place = pl.ds(pl.multiple_of((slot ^ mine) * chunk, chunk), chunk)
        out_ref[place, :] = ref[...].astype(F32) * factor


def run_forward(rows, coarse, levels, segment, args, pieces):
    tok, width = args[2].shape
    d_model = args[8].shape[1]
    head = len(pieces)
    blocks = tok // BLK
    keys_each = NBR * BLK + coarse
    tall = width // HDIM * BLK
    kept = [
        ((blocks, tall, keys_each), BF),
        ((blocks, tall, width), BF),
        ((blocks, tall, width), BF),
        ((blocks, tall, 1), F32),
        ((tok + 2 * RIM, width), BF),
        ((tok + 2 * RIM, width), BF),
    ]
    outs = call(
        functools.partial(forward_kernel, rows, levels),
        kept
        + [((head // 2 * tok, width), BF)] * 2
        + [((segment, d_model), BF)] * (1 << levels),
        [HBM] + [VMEM] * (9 + head),
        scratch=[
            pltpu.SMEM(args[0].shape, jnp.int32),
            pltpu.VMEM((tok, width), BF),
            pltpu.VMEM((width, d_model), BF),
            pltpu.SemaphoreType.DMA,
        ],
        flops=4 * blocks * tall * keys_each * width + 4 * tok * width * d_model,
        bytes_accessed=10_000_000,
    )(*args, *pieces)
    return outs[: len(kept)], outs[len(kept) :]


def run_backward(rows, neighbors, panel, saved):
    blocks, tall, width = saved[1].shape
    tok = blocks * BLK
    return call(
        functools.partial(backward_kernel, rows),
        [
            ((tok, width), BF),
            ((2 * tok, width), F32),
            ((2 * RIM, width), BF),
            ((2 * RIM, width), F32),
        ],
        [HBM] + [VMEM] * 7,
        scratch=[
            pltpu.SMEM(neighbors.shape, jnp.int32),
            pltpu.VMEM((tok + 2 * RIM, width), F32),
            pltpu.VMEM((tok + 2 * RIM, width), F32),
            pltpu.SemaphoreType.DMA,
        ],
        flops=8 * blocks * tall * saved[0].shape[2] * width,
        bytes_accessed=10_000_000,
    )(neighbors, panel, *saved)


def on_device(
    queries,
    keys,
    values,
    coarse_keys,
    coarse_values,
    neighbors,
    pool_map,
    coarse_mask,
    w_out,
    grad_mixed,
):
    tok, width = queries.shape
    rows = coarse_keys.shape[0]
    pix = lax.axis_size("pix")
    head = lax.axis_size("head")
    blocks = tok // BLK
    coarse = pix * rows
    d_model = head * width
    bits = bit_list(pix)
    head_bits = bit_list(head)
    levels = min(2, len(bits))
    pool_row = pool_map.reshape(1, tok)
    q_in, gm_in, w_in, mask_in = queries, grad_mixed, w_out, coarse_mask
    keys_hbm, values_hbm, ck_hbm, cv_hbm, pool_hbm, nbr_hbm = [
        pltpu.with_memory_space_constraint(x, pltpu.HBM)
        for x in (
            keys,
            values,
            coarse_keys,
            coarse_values,
            pool_row,
            neighbors,
        )
    ]
    across = head // 2
    slots = 1 << levels
    held = (pix // slots + across - 1) // across * rows
    chunk = width // slots
    segment = chunk + held

    k_own, v_own, panel, pool_own = call(
        prep_kernel,
        [((tok, width), BF), ((tok, width), BF), ((2 * rows, width), BF), ((1, tok), jnp.int32)],
        [HBM] * 5,
        scratch=[
            pltpu.VMEM((rows, width), BF),
            pltpu.VMEM((rows, width), BF),
            pltpu.SemaphoreType.DMA((5,)),
        ],
    )(keys_hbm, values_hbm, ck_hbm, cv_hbm, pool_hbm)
    grad_early, panel = lax.optimization_barrier((grad_mixed, panel))
    panel = gather_bits(panel, bits[:1])
    send_near, send_far = call(
        rim_kernel,
        [((2 * RIM, width), BF), ((2 * RIM, width), BF)],
        [VMEM] * 3,
        flops=3_000_000_000,
        bytes_accessed=4_000_000,
    )(k_own, v_own, panel)
    near = exchange(send_near, near_pairs(pix))
    late = (q_in, gm_in, w_in, mask_in)
    first = True
    for at in range(1, len(bits), 2):
        parts = gather_parts(panel, bits[at : at + 2])
        if first and len(parts) > 1:
            parts[1], send_far, *late = lax.optimization_barrier((parts[1], send_far, *late))
            first = False
        panel = jnp.concatenate(parts, 0)
    far = exchange(send_far, far_pairs(pix))
    q_own, gm_own, w_own, mask_own = call(
        load_kernel,
        [
            ((tok, width), BF),
            ((tok, width), BF),
            ((width, d_model), BF),
            (coarse_mask.shape, jnp.int32),
        ],
        [HBM] * 4,
        scratch=[pltpu.SemaphoreType.DMA((4,))],
        bytes_accessed=0,
    )(*[pltpu.with_memory_space_constraint(x, pltpu.HBM) for x in late])

    order = [grad_early]
    index = [0]
    for bit in reversed(head_bits):
        if len(order) > 1:
            order[0] = gm_own
            *order, near = lax.optimization_barrier((*order, near))
        order = order + [swap(piece, "head", bit) for piece in order]
        index = index + [i ^ bit for i in index]
    grads = [order[index.index(j)] for j in range(1, head)]
    (grad_attn,) = call(
        grad_kernel,
        [((tok, width), BF)],
        [VMEM] * (1 + head),
        flops=0,
        bytes_accessed=0,
    )(w_own, gm_own, *grads)

    saved, (mix_keep, mix_send, *segments) = run_forward(
        rows,
        coarse,
        levels,
        segment,
        (nbr_hbm, mask_own, q_own, k_own, v_own, near, far, panel, w_own, grad_attn),
        (gm_own, *grads),
    )
    grad_queries, own, to_near, to_far = run_backward(rows, nbr_hbm, panel, saved)

    got = [swap(segments[m], "pix", m) for m in range(1, slots)]
    *got, to_near = lax.optimization_barrier((*got, to_near))
    total = segments[0].astype(F32)
    for piece in got:
        total = total + piece.astype(F32)
    whole = total
    sent = lax.optimization_barrier(whole.astype(BF))
    (to_far,) = call(
        round_kernel,
        [((2 * RIM, width), BF)],
        [VMEM] * 2,
        flops=3_000_000_000,
        bytes_accessed=4_000_000,
    )(to_far, sent)
    cells = cut(whole[chunk:], rows, 2 * width, pix // slots)
    part = whole[:chunk]
    for bit in bits[levels:]:
        got = swap(sent, "pix", bit).astype(F32)
        part = part + got[:chunk]
        other = cut(got[chunk:], rows, 2 * width, len(cells))
        cells = [cells[t] + other[t ^ 1] for t in range(0, len(cells), 2)]
        if len(cells) > 1:
            empty = [jnp.zeros_like(cells[0])] * (-len(cells) % across)
            full = cells + empty
            lines = [
                jnp.concatenate(full[t : t + across], 1) for t in range(0, len(full), across)
            ]
            sent = jnp.concatenate([part] + lines, 0).astype(BF)
    coarse_grads = cells[0]
    part = part.astype(BF)
    part, coarse_grads = lax.optimization_barrier((part, coarse_grads))
    gathered_parts = [part] + [swap(part, "pix", m) for m in range(1, slots)]
    (grad_w_out,) = call(
        functools.partial(gw_kernel, levels, (tok * pix) ** (-0.5)),
        [((width, d_model), F32)],
        [VMEM] * slots,
        flops=0,
        bytes_accessed=6 * width * d_model,
    )(*gathered_parts)

    kept, sent = mix_keep, mix_send
    for bit in head_bits:
        total = kept.astype(F32) + swap(sent, "head", bit).astype(F32)
        if kept.shape[0] > tok:
            half = kept.shape[0] // 2
            kept, sent = total[:half], total[half:].astype(BF)
    mixed = total.astype(BF)

    got_near = exchange(to_near, near_pairs(pix))
    got_far = exchange(to_far, far_pairs(pix))
    grad_keys, grad_values, grad_ck, grad_cv = call(
        finish_kernel,
        [((tok, width), BF), ((tok, width), BF), ((rows, width), F32), ((rows, width), F32)],
        [VMEM] * 5,
        scratch=[pltpu.VMEM((tok, width), F32)],
        flops=3_000_000_000,
        bytes_accessed=16 * tok * width,
    )(own, got_near, got_far, coarse_grads, pool_own)
    return (mixed, grad_queries, grad_keys, grad_values, grad_ck, grad_cv, grad_w_out)


def solution(mesh):
    in_specs = (
        P("pix", "head"),
        P("pix", "head"),
        P("pix", "head"),
        P("pix", "head"),
        P("pix", "head"),
        P("pix", None),
        P("pix"),
        P("pix", None),
        P("head", None),
        P("pix", "head"),
    )
    out_specs = (
        P("pix", "head"),
        P("pix", "head"),
        P("pix", "head"),
        P("pix", "head"),
        P("pix", "head"),
        P("pix", "head"),
        P("head", None),
    )
    return jax.shard_map(
        on_device, mesh=mesh, in_specs=in_specs, out_specs=out_specs, check_vma=False
    )
```
